32 devices in a mesh: dp: 16 (over z, y, x), tensor: 2 (over core).
Axes of the slice: x: 2, y: 2, z: 4, core: 2. Of those that a mesh axis runs over, the one named last changes fastest.
Arguments:
- tokens: bfloat16 [16384, 1024], P(('dp', 'tensor')), may hold values from -6 to 6
- episode_lengths: int32 [16, 4], P('dp'), may hold values from 1 to 640, 1024 in all within a row
- attn_gain: float32 [1024], replicated, may hold values from 0.25 to 1.75
- attn_shift: float32 [1024], replicated, may hold values from -3 to 3
- proj_weight: bfloat16 [3, 1024, 1024], P(None, None, 'tensor'), may hold values from -0.1875 to 0.1875
- proj_bias: float32 [3, 1024], P(None, 'tensor'), may hold values from -2 to 2
- out_weight: bfloat16 [1024, 1024], P('tensor'), may hold values from -1.5 to 1.5
- out_bias: float32 [1024], replicated, may hold values from -2 to 2
- mlp_gain: float32 [1024], replicated, may hold values from 0.25 to 1.75
- mlp_shift: float32 [1024], replicated, may hold values from -3 to 3
- up_weight: bfloat16 [1024, 4096], P(None, 'tensor'), may hold values from -0.1875 to 0.1875
- up_bias: float32 [4096], P('tensor'), may hold values from -2 to 2
- down_weight: bfloat16 [4096, 1024], P('tensor'), may hold values from -0.1875 to 0.1875
- down_bias: float32 [1024], replicated, may hold values from -2 to 2
- cotangent: bfloat16 [16384, 1024], P(('dp', 'tensor')), may hold values from -6 to 6
Outputs:
- mixed: bfloat16 [16384, 1024], P(('dp', 'tensor'))
- grad_tokens: float32 [16384, 1024], P(('dp', 'tensor'))
- grad_attn_gain: float32 [1024], replicated
- grad_attn_shift: float32 [1024], replicated
- grad_proj_weight: float32 [3, 1024, 1024], P(None, 'dp', 'tensor')
- grad_proj_bias: float32 [3, 1024], replicated
- grad_out_weight: float32 [1024, 1024], P('tensor', 'dp')
- grad_out_bias: float32 [1024], replicated
- grad_mlp_gain: float32 [1024], replicated
- grad_mlp_shift: float32 [1024], replicated
- grad_up_weight: float32 [1024, 4096], P('dp', 'tensor')
- grad_up_bias: float32 [4096], replicated
- grad_down_weight: float32 [4096, 1024], P('tensor', 'dp')
- grad_down_bias: float32 [1024], replicated
The draws below stay inside these ranges and needn't reach their ends.
Inputs may be any that keep to these rules, and one draw needn't show every extreme that they name: `episode_lengths`: each row lists the lengths of the 4 episodes of one pack in order; a row sums to 1024 and its largest entry is exactly 640.
All inputs are finite; a program needn't handle non-finite values.
Results may differ from the reference program's by a relative error of at most 0.017.
Values may be sent and summed in bfloat16 or wider, within the bound.
A program may use at most 192 MiB of HBM per device.

```python
import math
import jax
import jax.numpy as jnp
import numpy as np
from jax import lax

D = 1024
HEADS = 16
HEAD = 64
FF = 4096
GRID = 16
EPISODES = 4
FRAME = 258
PACK = 1024
LONGEST = 640
TOKENS = 16384
N_DP = 16


def strengthened(entries, rng, source, target, parts, factor):
    def block_of(axis_at):
        return (jnp.arange(entries.shape[axis_at]) // (entries.shape[axis_at] // parts)).reshape((-1,) + (1,) * (entries.ndim - 1 - axis_at))

    near = jax.random.permutation(rng, parts)[block_of(target)]
    other_side = (block_of(target) + parts // 2) % parts
    return jnp.where((block_of(source) == near) | (block_of(source) == other_side), factor * entries, entries)


def steps_of(key, dims, cuts, smallest, high):
    level, own = 1.0, jax.random.fold_in(key, 6)
    for axis_at, blocks in cuts:
        steps = jnp.exp(jax.random.uniform(jax.random.fold_in(own, axis_at), (blocks,), jnp.float32, smallest / len(cuts), high / len(cuts)))
        level = level * jnp.repeat(steps, dims[axis_at] // blocks).reshape([-1 if axis == axis_at else 1 for axis in range(len(dims))])
    return level


def length_profile(amount, total, most, lean):
    weights = [(1 << 20) // math.isqrt(rank ** lean) + 1 for rank in range(2, amount + 1)]
    spare, holding = total - most - (amount - 1), [1] * (amount - 1)
    while spare > 0:
        free = [i for i in range(amount - 1) if holding[i] < most]
        whole, left = sum([weights[i] for i in free]), spare
        for i in free:
            more = min(most - holding[i], max(1, left * weights[i] // whole), spare)
            holding[i] = holding[i] + more
            spare = spare - more
    return np.array([most] + holding)


def uneven_parts(key, amount, total, bound, lean):
    if amount == 2:
        one = jax.random.randint(key, (), max(1, total - bound), min(bound, total - 1) + 1)
        return jnp.stack([one, total - one])
    tallies = jnp.asarray(length_profile(amount, total, bound, lean), jnp.int32)
    couples = (amount - 1) // 2
    giver, receiver = tallies[1:1 + 2 * couples:2], tallies[2:2 + 2 * couples:2]
    slack = jnp.minimum(giver - 1, bound - receiver)
    shifted = jax.random.randint(jax.random.fold_in(key, 1), (couples,), 0, 1 << 20) % (slack + 1)
    tallies = tallies.at[1:1 + 2 * couples:2].set(giver - shifted).at[2:2 + 2 * couples:2].set(receiver + shifted)
    return tallies[jax.random.permutation(jax.random.fold_in(key, 2), amount)]


def noise(stream_key, extent, scale, most, cuts=(), kind=jnp.bfloat16):
    values = scale * jax.random.normal(stream_key, extent, jnp.float32)
    if cuts:
        values = values * steps_of(stream_key, extent, cuts, -0.22, 0.18)
    return jnp.clip(values, -most, most).astype(kind)


def noise_with(rng, extent, scale, bound, split, heavy, held_as=jnp.bfloat16):
    array = scale * jax.random.normal(rng, extent, jnp.float32)
    if split:
        array = array * steps_of(rng, extent, split, -0.22, 0.18)
    return jnp.clip(strengthened(array, jax.random.fold_in(rng, 3), *heavy), -bound, bound).astype(held_as)


def setup_inputs(seed: int = 0) -> dict:
    arg_keys = jax.random.split(jax.random.key(seed), 16)
    return {
        "tokens": noise(arg_keys[0], (TOKENS, D), 1.0, 6.0, ((0, 32),)),
        "episode_lengths": jax.vmap(lambda own: uneven_parts(own, EPISODES, PACK, LONGEST, 2))(jax.random.split(arg_keys[1], N_DP)).reshape((N_DP, EPISODES)).astype(jnp.int32),
        "attn_gain": jnp.clip(1.0 + 0.15 * jax.random.normal(arg_keys[2], (D,), jnp.float32), 0.25, 1.75),
        "attn_shift": noise(arg_keys[3], (D,), 0.5, 3.0, (), jnp.float32),
        "proj_weight": noise(arg_keys[4], (3, D, D), D ** -0.5, 0.1875, ((2, 2),)),
        "proj_bias": noise(arg_keys[5], (3, D), 0.3, 2.0, ((1, 2),), jnp.float32),
        "out_weight": noise(arg_keys[6], (D, D), (D // 64) ** -0.5, 1.5, ((0, 2),)),
        "out_bias": noise(arg_keys[7], (D,), 0.3, 2.0, (), jnp.float32),
        "mlp_gain": jnp.clip(1.0 + 0.15 * jax.random.normal(arg_keys[8], (D,), jnp.float32), 0.25, 1.75),
        "mlp_shift": noise(arg_keys[9], (D,), 0.5, 3.0, (), jnp.float32),
        "up_weight": noise(arg_keys[10], (D, FF), D ** -0.5, 0.1875, ((1, 2),)),
        "up_bias": noise(arg_keys[11], (FF,), 0.3, 2.0, ((0, 2),), jnp.float32),
        "down_weight": noise(arg_keys[12], (FF, D), (FF // 4) ** -0.5, 0.1875, ((0, 2),)),
        "down_bias": noise(arg_keys[13], (D,), 0.3, 2.0, (), jnp.float32),
        "cotangent": noise_with(arg_keys[14], (TOKENS, D), 1.0, 6.0, ((0, 32),), (0, 1, 32, 2.75)),
    }


epsilon = 1e-06
exact_mode = lax.Precision.HIGHEST

@jax.custom_vjp
def low(v):
    return lax.optimization_barrier(v.astype(jnp.bfloat16)).astype(jnp.float32)

@jax.custom_vjp
def low_back(v):
    return v

def low_keep(v):
    return (low(v), None)

def low_pass(kept, grad):
    return (grad,)

def back_keep(v):
    return (v, None)

def back_low(kept, grad):
    return (low(grad),)
low.defvjp(low_keep, low_pass)
low_back.defvjp(back_keep, back_low)

def layer_norm(values, gain, shift):
    centre = values - lax.optimization_barrier(jnp.mean(values, axis=-1, keepdims=True))
    spread = lax.optimization_barrier(jnp.mean(centre * centre, axis=-1, keepdims=True))
    return centre * lax.rsqrt(spread + epsilon) * gain + shift

def rotate(values, time_pos, row_pos, col_pos):
    head_width = values.shape[-1]
    side_width = 2 * (head_width // 6)
    pieces = []
    offset = 0
    for section, where_pos in ((head_width - 2 * side_width, time_pos), (side_width, row_pos), (side_width, col_pos)):
        half_width = section // 2
        frequency = 10000.0 ** (-jnp.arange(half_width, dtype=jnp.float32) * 2.0 / section)
        angles = where_pos.astype(jnp.float32)[:, None] * frequency[None, :]
        cosine = jnp.cos(angles)[:, None, :]
        sine_part = jnp.sin(angles)[:, None, :]
        leading = values[..., offset:offset + half_width]
        second = values[..., offset + half_width:offset + section]
        pieces.append(leading * cosine - second * sine_part)
        pieces.append(second * cosine + leading * sine_part)
        offset = offset + section
    return jnp.concatenate(pieces, axis=-1)

def positions(lengths_row, count):
    lengths_row = lengths_row.astype(jnp.int32)
    ends = jnp.cumsum(lengths_row).astype(jnp.int32)
    starts = ends - lengths_row
    places = jnp.arange(count, dtype=jnp.int32)
    episode = lax.optimization_barrier(jnp.sum((places[None, :] >= ends[:, None]).astype(jnp.int32), axis=0)).astype(jnp.int32)
    member = episode[None, :] == jnp.arange(lengths_row.shape[0], dtype=jnp.int32)[:, None]
    begin = lax.optimization_barrier(jnp.sum(jnp.where(member, starts[:, None], 0), axis=0)).astype(jnp.int32)
    local_pos = places - begin
    frame_id = local_pos // FRAME
    within_frame = local_pos % FRAME
    patch_id = jnp.maximum(within_frame - 2, 0)
    row_pos = jnp.where(within_frame >= 2, patch_id // GRID, 0)
    col_pos = jnp.where(within_frame >= 2, patch_id % GRID, 0)
    return (episode, frame_id, row_pos, col_pos)

def attend_block(queries, key_rows, value_rows, episode_q, frame_q, episode_k, frame_k):
    scores = jnp.einsum('qhe,khe->hqk', queries, key_rows, precision=exact_mode)
    scores = low_back(scores)
    allowed = (episode_q[:, None] == episode_k[None, :]) & (frame_k[None, :] <= frame_q[:, None])
    scores = jnp.where(allowed[None], scores, -1e+30)
    highest = lax.optimization_barrier(jnp.max(scores, axis=-1, keepdims=True))
    raised = jnp.exp(scores - highest)
    attention = raised / lax.optimization_barrier(jnp.sum(raised, axis=-1, keepdims=True))
    return jnp.einsum('hqk,khe->qhe', low(attention), value_rows, precision=exact_mode)

def pack_forward(params, tokens_pack, episode, frame_id, row_pos, col_pos):
    attn_gain, attn_shift, proj_weight, proj_bias, out_weight, out_bias, mlp_gain, mlp_shift, up_weight, up_bias, down_weight, down_bias = params
    pack_rows = tokens_pack.shape[0]
    normed_one = low(layer_norm(tokens_pack, attn_gain, attn_shift))
    project = jnp.einsum('pd,cde->cpe', normed_one, proj_weight, precision=exact_mode) + proj_bias[:, None, :]
    project = low_back(project)
    scale = HEAD ** (-0.5)
    queries = low(low_back(rotate(project[0].reshape(pack_rows, HEADS, HEAD), frame_id, row_pos, col_pos) * scale))
    key_rows = low(low_back(rotate(project[1].reshape(pack_rows, HEADS, HEAD), frame_id, row_pos, col_pos)))
    value_rows = low(project[2].reshape(pack_rows, HEADS, HEAD))
    block = min(512, pack_rows)

    def one_block(index):
        start = index * block
        q_block = lax.dynamic_slice_in_dim(queries, start, block, 0)
        episode_q = lax.dynamic_slice_in_dim(episode, start, block, 0)
        frame_q = lax.dynamic_slice_in_dim(frame_id, start, block, 0)
        return attend_block(q_block, key_rows, value_rows, episode_q, frame_q, episode, frame_id)
    blocks = lax.map(jax.checkpoint(one_block), jnp.arange(pack_rows // block, dtype=jnp.int32))
    attended = low(low_back(blocks.reshape(pack_rows, HEADS * HEAD)))
    branch_one = low_back(jnp.dot(attended, out_weight, precision=exact_mode) + out_bias)
    middle = tokens_pack + branch_one
    normed_two = low(layer_norm(middle, mlp_gain, mlp_shift))
    hidden = low_back(jnp.dot(normed_two, up_weight, precision=exact_mode) + up_bias)
    active = low(jax.nn.gelu(hidden, approximate=False))
    branch_two = low_back(jnp.dot(active, down_weight, precision=exact_mode) + down_bias)
    return middle + branch_two

def reference(tokens, episode_lengths, attn_gain, attn_shift, proj_weight, proj_bias, out_weight, out_bias, mlp_gain, mlp_shift, up_weight, up_bias, down_weight, down_bias, cotangent):
    params = tuple((item.astype(jnp.float32) for item in (attn_gain, attn_shift, proj_weight, proj_bias, out_weight, out_bias, mlp_gain, mlp_shift, up_weight, up_bias, down_weight, down_bias)))
    pack_count = episode_lengths.shape[0]
    width = tokens.shape[1]
    token_packs = tokens.astype(jnp.float32).reshape(pack_count, PACK, width)
    cot_packs = cotangent.astype(jnp.float32).reshape(pack_count, PACK, width)

    def one_pack(totals, inputs):
        tokens_pack, cot_pack, lengths_row = inputs
        episode, frame_id, row_pos, col_pos = positions(lengths_row, PACK)

        def forward(params_in, tokens_in):
            return pack_forward(params_in, tokens_in, episode, frame_id, row_pos, col_pos)
        output, pullback = jax.vjp(forward, params, tokens_pack)
        grad_params, grad_input = pullback(cot_pack)
        totals = jax.tree.map(jnp.add, totals, grad_params)
        return (totals, (output.astype(jnp.bfloat16), grad_input))
    zeros = jax.tree.map(jnp.zeros_like, params)
    totals, (outputs, grad_inputs) = lax.scan(one_pack, zeros, (token_packs, cot_packs, episode_lengths))
    return (outputs.reshape(pack_count * PACK, width), grad_inputs.reshape(pack_count * PACK, width), totals[0], totals[1], totals[2], totals[3], totals[4], totals[5], totals[6], totals[7], totals[8], totals[9], totals[10], totals[11])
```

```python
import functools
import math

import jax
import jax.numpy as jnp
import ml_dtypes
import numpy as np
from jax import lax
from jax.experimental import pallas as pl
from jax.experimental.pallas import tpu as pltpu
from jax.sharding import PartitionSpec as P

HEAD = 64
GRID = 16
FRAME = 258
EPS = 1e-6
LANES = 128
FC = 256
MESH = pl.DeviceIdType.MESH
F32 = jnp.float32
BF = jnp.bfloat16
NEG = -1e30
FRAMES = 4
TERM = 16


def nn(a, b):
    return jnp.dot(a, b, preferred_element_type=F32)


def nt(a, b):
    return lax.dot_general(a, b, (((1,), (1,)), ((), ())), preferred_element_type=F32)


def rope_tables():
    side = 2 * (HEAD // 6)
    sections = (HEAD - 2 * side, side, side)
    cos = np.zeros((FRAMES + 2 * GRID, HEAD), np.float64)
    sin = np.zeros((FRAMES + 2 * GRID, HEAD), np.float64)
    lane, row = 0, 0
    for width, count in zip(sections, (FRAMES, GRID, GRID)):
        half = width // 2
        freq = np.float32(10000.0) ** (-np.arange(half, dtype=np.float32) * np.float32(2.0) / np.float32(width))
        angle = (np.arange(count, dtype=np.float32)[:, None] * freq.astype(np.float32)[None, :]).astype(np.float64)
        cos[row : row + count, lane : lane + half] = np.cos(angle)
        cos[row : row + count, lane + half : lane + width] = np.cos(angle)
        sin[row : row + count, lane : lane + half] = -np.sin(angle)
        sin[row : row + count, lane + half : lane + width] = np.sin(angle)
        lane, row = lane + width, row + count
    both = np.concatenate([cos, cos, sin, sin], axis=1).astype(np.float32)
    out = np.zeros((LANES, 4 * HEAD), ml_dtypes.bfloat16)
    rest, n = both, both.shape[0]
    for term in range(3):
        part = rest.astype(ml_dtypes.bfloat16)
        out[term * n : (term + 1) * n] = part
        rest = rest - part.astype(np.float32)
    return out


def partner_of(x, lane):
    side = 2 * (HEAD // 6)
    first = HEAD - 2 * side
    a, b = first // 2, side // 2
    within = lane % HEAD
    past = (within - first) % side
    up_a = pltpu.roll(x, LANES - a, 1)
    down_a = pltpu.roll(x, a, 1)
    up_b = pltpu.roll(x, LANES - b, 1)
    down_b = pltpu.roll(x, b, 1)
    in_first = jnp.where(within < a, up_a, down_a)
    in_side = jnp.where(past < b, up_b, down_b)
    return jnp.where(within < first, in_first, in_side)


def split3(x):
    hi = x.astype(BF).astype(F32)
    mid = (x - hi).astype(BF).astype(F32)
    return hi, mid, x - hi - mid


def kernel(
    dp, tok_h, cot_h, pw_h, ow_h, uw_h, dw_h, lens, gain1, shift1, pbias, obias, gain2, shift2, ubias, dbias, table,
    mixed_h, gtok_h, gout, small, U, DN, OW, TOKX, N1, T1, T2, CG, N2, QA, K, V, ATT, ACT, GH, MID, X1, S1,
    ONE, QF, KF, SB, SBR, G, *rest,
):
    stages = dp.bit_length() - 1
    RM, RP = rest[:stages], rest[stages : 2 * stages]
    m_send, m_recv, p_send, p_recv, x_send, x_recv, b_send, b_recv, loads = rest[2 * stages :]
    T = tok_h.shape[0]
    D = tok_h.shape[1]
    R = 2 * T
    E = OW.shape[0]
    F = DN.shape[0]
    pairs = E // LANES
    nf = F // FC
    low = stages - 4
    unit = 1 << low
    me = lax.axis_index("dp")
    core = lax.axis_index("tensor")
    lane = lax.broadcasted_iota(jnp.int32, (1, LANES), 1)

    def bit_of(stride):
        return (me // stride) % 2

    def partner(stride):
        return me + (1 - 2 * bit_of(stride)) * stride

    def load(src, dst, k):
        return pltpu.make_async_copy(src, dst, loads.at[k])

    tok_load = load(tok_h, TOKX, 0)
    cot_load = load(cot_h, CG.at[pl.ds(0, T)], 1)
    pw_loads = [load(pw_h.at[c], U.at[:, pl.ds(c * E, E)], 2 + c) for c in range(3)]
    ow_load = load(ow_h, OW, 5)
    uw_load = load(uw_h, U, 6)
    dw_load = load(dw_h, DN, 7)
    pw_again = [load(pw_h.at[c], U.at[:, pl.ds(c * E, E)], 8 + c) for c in range(3)]
    tok_again = load(tok_h, N2.at[pl.ds(0, T)], 11)
    mixed_store = load(N2.at[pl.ds(0, T)], mixed_h, 12)
    gtok_store = load(MID, gtok_h, 13)
    tok_load.start()
    cot_load.start()
    for c in pw_loads:
        c.start()
    ow_load.start()
    dw_load.start()

    barrier = pltpu.get_barrier_semaphore()
    peers = [(partner(1 << b), core) for b in range(stages)] + [(me, 1 - core)]
    for who in peers:
        pl.semaphore_signal(barrier, inc=1, device_id=who, device_id_type=MESH)
    pl.semaphore_wait(barrier, len(peers))

    def cross(src, dst, k):
        return pltpu.make_async_remote_copy(
            src_ref=src, dst_ref=dst, send_sem=x_send.at[k], recv_sem=x_recv.at[k],
            device_id=(me, 1 - core), device_id_type=MESH,
        )

    half = T // 2

    def turned(dst, src, first, count):
        @pl.loop(first // 256, (first + count) // 256)
        def _(m):
            rows = pl.ds(pl.multiple_of(m * 256, 256), 256)
            dst[:, rows] = src[rows].T

    def cross_rows(src, s0, dst, d0, base, m):
        return cross(src.at[pl.ds(s0 + m * half, half)], dst.at[pl.ds(d0 + m * half, half)], base + m)

    def order_of(kind, par):
        where = {"x": unit * (1 + par), "y": unit * (2 - par), "z": unit * 4, "Z": unit * 8}
        return [where[k] for k in kind + "Z"] + [1 << b for b in reversed(range(low))]

    def places_of(kind, par):
        w = {k: 8 >> i for i, k in enumerate(kind + "Z")}
        return (w["x"] + par * (w["y"] - w["x"]), w["y"] + par * (w["x"] - w["y"]), w["z"], w["Z"])

    def g_view(fam, c):
        if fam == "M":
            return G.at[c % 8]
        if fam == "O":
            return G.at[8 + c]
        p, k = c
        return G.at[p + 4 * (k // 2), :, pl.ds((k % 2) * LANES, LANES)]

    def slot(fam, c):
        if fam == "M":
            return RM, c, m_send, m_recv
        if fam == "O":
            return RM, 2 * nf + c, m_send, m_recv
        return RP, 3 * c[0] + c[1], p_send, p_recv

    block = D // 16

    def put(fam, c, value, row0, kind, par):
        w = places_of(kind, par)
        view = g_view(fam, c)
        for b in range(value.shape[0] // block):
            n = row0 * (value.shape[0] // block) + b
            place = ((n % 2) * w[0] + ((n // 2) % 2) * w[1] + ((n // 4) % 2) * w[2] + (n // 8) * w[3]) * block
            view[pl.ds(pl.multiple_of(place, block), block), :] = value[b * block : (b + 1) * block].astype(BF)

    def rs_parts(fam, c, s, order):
        R_, at, ss, rr = slot(fam, c)
        view = g_view(fam, c) if s == 0 else R_[s - 1].at[at]
        n = D >> s
        h = n // 2
        bit = bit_of(order[s])
        if h >= 16:
            src = view.at[pl.ds(pl.multiple_of((1 - bit) * h, 16), h)]
            keep = view.at[pl.ds(pl.multiple_of(bit * h, 16), h)]
        else:
            src = keep = view
        copy = pltpu.make_async_remote_copy(
            src_ref=src, dst_ref=R_[s].at[at], send_sem=ss.at[at, s], recv_sem=rr.at[at, s],
            device_id=(partner(order[s]), core), device_id_type=MESH,
        )
        return copy, keep, R_[s].at[at], bit, h

    def columns_of(fam, c):
        if fam == "M":
            return pl.multiple_of((c % 2) * F + (c // 2) * FC, FC), FC
        if fam == "O":
            return 2 * F + c * FC, FC
        return pl.multiple_of(2 * F + E + c[1] * E + c[0] * LANES, LANES), LANES

    def rs_start(fam, c, s, order):
        rs_parts(fam, c, s, order)[0].start()

    def rs_step(fam, c, s, order):
        copy, keep, landed, bit, h = rs_parts(fam, c, s, order)
        copy.wait()
        if s < stages - 1:
            n = landed.shape[0]
            piece = min(n, 64)
            if n == piece:
                landed[...] = landed[...] + keep[...]
            else:
                @pl.loop(0, n // piece)
                def _(q):
                    at = pl.ds(pl.multiple_of(q * piece, piece), piece)
                    landed[at] = landed[at] + keep[at]

            rs_start(fam, c, s + 1, order)
        else:
            total = landed[...].astype(F32) + keep[...].astype(F32)
            if h < 16:
                total = jnp.where(bit == 1, total[8:], total[:8])
            start, width = columns_of(fam, c)
            gout[:, pl.ds(start, width)] = total

    M_KINDS = ("xyz", "yzx", "zxy", "yxz")

    def m_kind(e, k):
        return M_KINDS[2 * e + k]

    def m_par(i):
        return (i // 2) % 2

    def m_steps(i, e, s):
        for k in range(2):
            rs_step("M", 2 * i + k, s, order_of(m_kind(e, k), m_par(i)))

    O_KINDS = ("xzy", "zyx")
    P_KINDS = ("xyz", "yzx", "zxy")

    def normed(x):
        centre = x - jnp.mean(x, axis=1, keepdims=True)
        inv = lax.rsqrt(jnp.mean(centre * centre, axis=1, keepdims=True) + EPS)
        return centre * inv, inv

    tok_load.wait()

    @pl.loop(0, 2)
    def _(m):
        @pl.loop(0, half // 128)
        def _(q):
            rows = pl.ds(m * half + q * 128, 128)
            x = TOKX[rows].astype(F32)
            N1[rows] = (normed(x)[0] * gain1[...] + shift1[...]).astype(BF)

        cross_rows(N1, 0, N1, T, 1, m).start()

    cot_load.wait()
    cot_send = cross(CG.at[pl.ds(0, T)], CG.at[pl.ds(T, T)], 0)
    cot_send.start()

    @pl.loop(0, R // 256)
    def _(m):
        row = lax.broadcasted_iota(jnp.int32, (256, 1), 0) + m * 256
        place = (row + core * T) % R
        begin = jnp.zeros((256, 1), jnp.int32)
        episode = jnp.zeros((256, 1), jnp.int32)
        end = jnp.int32(0)
        for e in range(lens.shape[1] - 1):
            end = end + lens[0, e]
            begin = jnp.where(place >= end, end, begin)
            episode = jnp.where(place >= end, e + 1, episode)
        local = place - begin
        frame = jnp.zeros((256, 1), jnp.int32)
        for k in range(1, FRAMES):
            frame = jnp.where(local >= k * FRAME, k, frame)
        inside = local - frame * FRAME
        patch = jnp.maximum(inside - 2, 0)
        row_pos = jnp.where(inside >= 2, patch // GRID, 0)
        col_pos = jnp.where(inside >= 2, patch % GRID, 0)
        n = FRAMES + 2 * GRID
        spot = lane % n
        hit = (spot == frame) | (spot == FRAMES + row_pos) | (spot == FRAMES + GRID + col_pos)
        hit = hit & (lane < 3 * n)
        rows = pl.ds(m * 256, 256)
        ONE[rows] = jnp.where(hit, 1.0, 0.0).astype(BF)
        feature = lane % HEAD
        counted = (feature // FRAMES == episode) & (feature % FRAMES <= frame)
        is_class = feature < TERM
        QF[rows] = jnp.where(is_class & jnp.logical_not(counted), NEG, 0.0).astype(BF)
        ones = (feature == episode * FRAMES + frame) | ((feature >= TERM) & (feature < TERM + 3))
        KF[rows] = jnp.where(ones, 1.0, 0.0).astype(BF)

    def rotary(rows):
        both = nn(ONE[rows], table[...])
        return both[:, :LANES], both[:, LANES:]

    for c in pw_loads:
        c.wait()

    def project(m):
        rows = pl.ds(m * 256, 256)
        x = N1[rows]
        cos, sin = rotary(rows)
        q = nn(x, U[:, 0:E]) + pbias[:, 0:E]
        for p in range(pairs):
            v = q[:, p * LANES : (p + 1) * LANES]
            v = ((v * cos + partner_of(v, lane) * sin) * HEAD**-0.5).astype(BF)
            QA[2 * p, rows] = jnp.where(lane < HEAD, v, QF[rows])
            QA[2 * p + 1, rows] = jnp.where(lane >= HEAD, v, QF[rows])
        k = nn(x, U[:, E : 2 * E]) + pbias[:, E : 2 * E]
        for p in range(pairs):
            v = k[:, p * LANES : (p + 1) * LANES]
            K[rows, p * LANES : (p + 1) * LANES] = (v * cos + partner_of(v, lane) * sin).astype(BF)
        V[rows] = (nn(x, U[:, 2 * E : 3 * E]) + pbias[:, 2 * E : 3 * E]).astype(BF)

    @pl.loop(0, 2)
    def _(m):
        project(m)

    turned(T1, CG, 0, T)

    @pl.loop(0, 2)
    def _(m):
        cross_rows(N1, 0, N1, T, 1, m).wait()
        project(2 + m)

    uw_load.start()

    def mine(e):
        return lane < HEAD if e == 0 else lane >= HEAD

    def key_sets(p, box):
        cols = pl.ds(pl.multiple_of(p * LANES, LANES), LANES)
        for e in range(2):
            box[:, e * LANES : (e + 1) * LANES] = jnp.where(mine(e), K[:, cols], KF[...])
            box[:, (2 + e) * LANES : (3 + e) * LANES] = jnp.where(mine(e), V[:, cols], jnp.ones((), BF))

    def attend(first):
        @pl.loop(0, pairs)
        def _(p):
            key_sets(p, T2)

            @pl.loop(0, T // 256)
            def _(b):
                rows = pl.ds(first + b * 256, 256)
                parts = []
                for e in range(2):
                    qa = QA[2 * p + e, rows]
                    s = nt(qa, T2[:, e * LANES : (e + 1) * LANES])
                    top = jnp.max(s, axis=1, keepdims=True)
                    w = jnp.exp(s - top).astype(BF)
                    o = nn(w, T2[:, (2 + e) * LANES : (3 + e) * LANES])
                    parts.append(o / pltpu.roll(o, HEAD, 1))
                    total = jnp.where(mine(e), 1.0, o)
                    hi, mid, lo = split3(top + jnp.log(total))
                    feature = lane % HEAD
                    terms = jnp.where(feature == TERM, -hi, jnp.where(feature == TERM + 1, -mid, -lo)).astype(BF)
                    is_term = (feature >= TERM) & (feature < TERM + 3) & jnp.logical_not(mine(e))
                    QA[2 * p + e, rows] = jnp.where(is_term, terms, qa)
                ATT[rows, pl.ds(pl.multiple_of(p * LANES, LANES), LANES)] = jnp.where(
                    lane < HEAD, parts[0], parts[1]
                ).astype(BF)

    attend(T)
    ow_load.wait()

    @pl.loop(0, 2)
    def _(m):
        rows = pl.ds(m * half, half)
        S1[rows] = nn(ATT[pl.ds(T + m * half, half)], OW[...]).astype(BF)
        cross_rows(S1, 0, X1, 0, 3, m).start()

    attend(0)

    @pl.loop(0, 2)
    def _(m):
        rows = pl.ds(m * half, half)
        MID[rows] = nn(ATT[rows], OW[...])
        cross_rows(S1, 0, X1, 0, 3, m).wait()

        @pl.loop(0, half // 128)
        def _(q):
            rows = pl.ds(m * half + q * 128, 128)
            mid = TOKX[rows].astype(F32) + (MID[rows] + X1[rows].astype(F32) + obias[...])
            MID[rows] = mid
            N2[rows] = (normed(mid)[0] * gain2[...] + shift2[...]).astype(BF)

        cross_rows(N2, 0, N2, T, 5, m).start()

    SB[...] = jnp.zeros_like(SB)
    SB[12:13] = jnp.sum(CG[0:T].astype(F32), axis=0, keepdims=True)
    turned(T2, N2, 0, T)
    cot_send.wait()
    turned(T1, CG, T, T)

    @pl.loop(0, 2)
    def _(m):
        cross_rows(N2, 0, N2, T, 5, m).wait()

    turned(T2, N2, T, T)
    uw_load.wait()
    dw_load.wait()

    ones8 = jnp.ones((8, R), BF)

    def hidden_chunk(i, e):
        cols = pl.ds(pl.multiple_of(i * FC, FC), FC)

        @pl.loop(0, R // 256)
        def _(m):
            rows = pl.ds(m * 256, 256)
            h = nn(N2[rows], U[:, cols]) + ubias[:, cols]
            cdf = 0.5 + 0.5 * lax.erf(h * math.sqrt(0.5))
            ACT[rows, cols] = (h * cdf).astype(BF)
            slope = cdf + h * jnp.exp(h * h * -0.5) * (1.0 / math.sqrt(2 * math.pi))
            GH[rows, cols] = (nt(CG[rows], DN[cols]) * slope).astype(BF)

        for k, (left, right) in enumerate(((T1, ACT), (T2, GH))):
            @pl.loop(0, D // 256)
            def _(m):
                put("M", 2 * i + k, nn(left[pl.ds(m * 256, 256)], right[:, cols]), m, m_kind(e, k), m_par(i))

            rs_start("M", 2 * i + k, 0, order_of(m_kind(e, k), m_par(i)))

        sums = nn(ones8, GH[:, cols])
        per = D // FC
        SB[pl.ds(8 + core * (F // D) + i // per, 1), pl.ds(pl.multiple_of((i % per) * FC, FC), FC)] = sums[0:1]

    @pl.loop(0, nf // 2)
    def _(j):
        for e in range(2):
            i = 2 * j + e
            hidden_chunk(i, e)
            for s in range(stages):
                lag = LAGS[s]
                if lag < nf:
                    @pl.when(i >= lag)
                    def _():
                        m_steps(i - lag, (e - lag) % 2, s)

    left = [(i + LAGS[s], -s, i, s) for s in range(stages) for i in range(nf) if i + LAGS[s] >= nf]
    left = [(i, s) for _, _, i, s in sorted(left)]

    def drain(count):
        for _ in range(min(count, len(left))):
            i, s = left.pop(0)
            m_steps(i, i % 2, s)

    def norm_back(g, x, gain, row):
        xhat, inv = normed(x)
        SB[row : row + 1] += jnp.sum(g * xhat, axis=0, keepdims=True)
        SB[row + 1 : row + 2] += jnp.sum(g, axis=0, keepdims=True)
        gx = g * gain
        a = jnp.mean(gx, axis=1, keepdims=True)
        b = jnp.mean(gx * xhat, axis=1, keepdims=True)
        return inv * (gx - a - xhat * b)

    @pl.loop(0, 2)
    def _(m):
        S1[pl.ds(m * half, half)] = nt(GH[pl.ds(T + m * half, half)], U[...]).astype(BF)
        cross_rows(S1, 0, X1, 0, 7, m).start()

    drain(DRAIN[0])

    @pl.loop(0, 2)
    def _(m):
        rows = pl.ds(m * half, half)
        own = nt(GH[rows], U[...])
        cross_rows(S1, 0, X1, 0, 7, m).wait()
        for q in range(half // 128):
            at = pl.ds(m * half + q * 128, 128)
            g = own[q * 128 : (q + 1) * 128] + X1[at].astype(F32)
            total = CG[at].astype(F32) + norm_back(g, MID[at], gain2[...], 6)
            high = total.astype(BF)
            CG[at] = high
            TOKX[at] = (total - high.astype(F32)).astype(BF)
            SB[5:6] += jnp.sum(high.astype(F32), axis=0, keepdims=True)
        cross_rows(CG, 0, CG, T, 9, m).start()

    for c in pw_again:
        c.start()

    @pl.loop(0, 2)
    def _(m):
        S1[pl.ds(m * half, half)] = nn(ACT[pl.ds(T + m * half, half)], DN[...]).astype(BF)
        cross_rows(S1, 0, N2, T, 11, m).start()

    drain(DRAIN[1])

    def grad_attended(m):
        rows = pl.ds(m * half, half)
        GH[rows, 0:E] = nt(CG[rows], OW[...]).astype(BF)

    @pl.loop(0, 2)
    def _(m):
        grad_attended(m)

    turned(T1, CG, 0, T)

    @pl.loop(0, 2)
    def _(m):
        cross_rows(CG, 0, CG, T, 9, m).wait()
        grad_attended(2 + m)

    turned(T1, CG, T, T)
    for c in range(2):
        @pl.loop(0, D // 256)
        def _(m):
            put("O", c, nn(T1[pl.ds(m * 256, 256)], ATT[:, c * FC : (c + 1) * FC]), m, O_KINDS[c], 0)

        rs_start("O", c, 0, order_of(O_KINDS[c], 0))
    drain(DRAIN[2])
    turned(T2, N1, 0, R)

    @pl.loop(0, 2)
    def _(m):
        rows = pl.ds(m * half, half)
        own = nn(ACT[rows], DN[...])
        cross_rows(S1, 0, N2, T, 11, m).wait()
        N2[rows] = (MID[rows] + (own + N2[pl.ds(T + m * half, half)].astype(F32) + dbias[...])).astype(BF)

    mixed_store.start()
    drain(DRAIN[3])

    def p_step(p, s):
        for k in range(3):
            rs_step("P", (p, k), s, order_of(P_KINDS[k], 0))

    def o_step(s):
        for c in range(2):
            rs_step("O", c, s, order_of(O_KINDS[c], 0))

    def pair_grads(b):
        rows = pl.ds((b % 2) * 256, 256)
        return [(rows, pl.ds(pl.multiple_of((b // 2) * 2 * LANES + k * LANES, LANES), LANES)) for k in range(2)]

    def query_grads(a, e):
        return pl.ds(a * LANES + e * HEAD, HEAD), pl.ds(D // 2, T)

    plan = []
    for _ in range(pairs):
        mine_now = left[: DRAIN[4]]
        del left[: DRAIN[4]]
        plan.append(mine_now)

    @pl.loop(0, pairs)
    def _(p):
        cols = pl.ds(pl.multiple_of(p * LANES, LANES), LANES)
        key_sets(p, T1)
        N1[0:LANES] = K[:, cols].T
        for e in range(2):
            @pl.loop(0, R // 256)
            def _(b):
                rows = pl.ds(b * 256, 256)
                g = GH[rows, cols]
                both = g.astype(F32) * ATT[rows, cols].astype(F32)
                inner = jnp.sum(jnp.where(mine(e), both, 0.0), axis=1, keepdims=True)
                hi, mid, lo = split3(inner)
                feature = lane % HEAD
                terms = jnp.where(feature == TERM, -hi, jnp.where(feature == TERM + 1, -mid, -lo))
                is_term = (feature >= TERM) & (feature < TERM + 3)
                terms = jnp.where(is_term, terms, 0.0).astype(BF)
                T1[rows, (4 + e) * LANES : (5 + e) * LANES] = jnp.where(mine(e), g, terms)

        for e in range(2):
            for a in range(2):
                MID[query_grads(a, e)] = jnp.zeros((HEAD, T), F32)

            @pl.loop(0, R // 256)
            def _(b):
                rows = pl.ds(b * 256, 256)
                dk = dv = 0.0
                for a in range(2):
                    across = pl.ds(a * T, T)
                    qa = QA[2 * p + e, across]
                    ga = T1[across, (4 + e) * LANES : (5 + e) * LANES]
                    w = jnp.exp(nt(T1[rows, e * LANES : (e + 1) * LANES], qa))
                    ds = (w * nt(T1[rows, (2 + e) * LANES : (3 + e) * LANES], ga)).astype(BF)
                    dv += nn(w.astype(BF), ga)
                    dk += nn(ds, qa)
                    MID[query_grads(a, e)] += nn(N1[e * HEAD : (e + 1) * HEAD, rows], ds)
                for at, g in zip(pair_grads(b), (dk, dv)):
                    MID[at] = g if e == 0 else jnp.where(mine(1), g, MID[at])

            for q, todo in enumerate(plan):
                here = todo[len(todo) // 2 :] if e else todo[: len(todo) // 2]
                if here:
                    @pl.when(p == q)
                    def _():
                        for i, s in here:
                            m_steps(i, i % 2, s)

        @pl.loop(0, R // 256)
        def _(b):
            rows = pl.ds(b * 256, 256)
            cos, sin = rotary(rows)
            turn = MID[pl.ds((b // 2) * LANES, LANES), pl.ds(pl.multiple_of(D // 2 + (b % 2) * 256, 256), 256)]

            def back(g):
                g = g.astype(BF).astype(F32)
                return g * cos - partner_of(g, lane) * sin

            parts = (
                back(turn.T) * HEAD**-0.5,
                *(f(MID[at]) for f, at in zip((back, lambda g: g), pair_grads(b))),
            )
            for c, part in enumerate(parts):
                GH[rows, pl.ds(pl.multiple_of(E + c * E + p * LANES, LANES), LANES)] = part.astype(BF)

        for c in range(3):
            own_cols = pl.ds(pl.multiple_of(E + c * E + p * LANES, LANES), LANES)
            at = core * E + p * LANES
            SB[2 + c : 3 + c, pl.ds(pl.multiple_of(at, LANES), LANES)] = nn(ones8, GH[:, own_cols])[0:1]

            @pl.loop(0, D // 256)
            def _(m):
                put("P", (p, c), nn(T2[pl.ds(m * 256, 256)], GH[:, own_cols]), m, P_KINDS[c], 0)

            rs_start("P", (p, c), 0, order_of(P_KINDS[c], 0))

        for s in range(stages):
            if s + 1 < pairs:
                @pl.when(p == s + 1)
                def _():
                    o_step(s)

            if P_LAGS[s] < pairs:
                @pl.when(p >= P_LAGS[s])
                def _():
                    p_step(p - P_LAGS[s], s)

    for c in pw_again:
        c.wait()
    mixed_store.wait()
    tok_again.start()

    @pl.loop(0, 2)
    def _(m):
        S1[pl.ds(m * half, half)] = nt(GH[pl.ds(T + m * half, half), E : 4 * E], U[:, : 3 * E]).astype(BF)
        cross_rows(S1, 0, X1, 0, 13, m).start()

    drain(len(left))
    tok_again.wait()

    @pl.loop(0, 2)
    def _(m):
        rows = pl.ds(m * half, half)
        own = nt(GH[rows, E : 4 * E], U[:, : 3 * E])
        cross_rows(S1, 0, X1, 0, 13, m).wait()
        for q in range(half // 128):
            at = pl.ds(m * half + q * 128, 128)
            g = own[q * 128 : (q + 1) * 128] + X1[at].astype(F32)
            before = CG[at].astype(F32) + TOKX[at].astype(F32)
            MID[at] = before + norm_back(g, N2[at].astype(F32), gain1[...], 0)

    gtok_store.start()

    later = [(s + 1, s, "O", 0) for s in range(stages) if s + 1 >= pairs]
    later += [(p + P_LAGS[s], s, "P", p) for s in range(stages) for p in range(pairs) if p + P_LAGS[s] >= pairs]
    later.sort(key=lambda z: (z[0], -z[1]))
    per = -(-len(later) // (stages + 1))

    def sums(s):
        who = (partner(1 << s), core) if s < stages else (me, 1 - core)
        return pltpu.make_async_remote_copy(
            src_ref=SB, dst_ref=SBR.at[s], send_sem=b_send.at[s], recv_sem=b_recv.at[s],
            device_id=who, device_id_type=MESH,
        )

    for s in range(stages + 1):
        sums(s).start()
        for _, st, fam, p in later[s * per : (s + 1) * per]:
            if fam == "O":
                o_step(st)
            else:
                p_step(p, st)
        sums(s).wait()
        SB[...] = SB[...] + SBR[s]
    small[...] = SB[...]
    gtok_store.wait()


LAGS = (1, 2, 3, 4, 5, 6, 7)
P_LAGS = (1, 2, 3, 4, 5, 6, 7)
DRAIN = (1, 2, 2, 1, 3)


def on_device(
    tokens, episode_lengths, attn_gain, attn_shift, proj_weight, proj_bias, out_weight, out_bias,
    mlp_gain, mlp_shift, up_weight, up_bias, down_weight, down_bias, cotangent,
):
    dp = lax.axis_size("dp")
    stages = dp.bit_length() - 1
    T, D = tokens.shape
    R = 2 * T
    E = proj_weight.shape[2]
    F = up_weight.shape[1]
    pairs = E // LANES
    nf = F // FC
    columns = 2 * F + 4 * E
    row = lambda v: v.reshape(1, -1).astype(F32)
    rows_at = [max(D >> (s + 1), 16) for s in range(stages)]
    vmem = pl.BlockSpec(memory_space=pltpu.VMEM)
    hbm = pl.BlockSpec(memory_space=pl.ANY)
    smem = pl.BlockSpec(memory_space=pltpu.SMEM)
    dma = pltpu.SemaphoreType.DMA
    scratch = [
        pltpu.VMEM((D, F), BF),
        pltpu.VMEM((F, D), BF),
        pltpu.VMEM((E, D), BF),
        pltpu.VMEM((T, D), BF),
        pltpu.VMEM((R, D), BF),
        pltpu.VMEM((D, R), BF),
        pltpu.VMEM((D, R), BF),
        pltpu.VMEM((R, D), BF),
        pltpu.VMEM((R, D), BF),
        pltpu.VMEM((2 * pairs, R, LANES), BF),
        pltpu.VMEM((R, E), BF),
        pltpu.VMEM((R, E), BF),
        pltpu.VMEM((R, E), BF),
        pltpu.VMEM((R, F), BF),
        pltpu.VMEM((R, F), BF),
        pltpu.VMEM((T, D), F32),
        pltpu.VMEM((T, D), BF),
        pltpu.VMEM((T, D), BF),
        pltpu.VMEM((R, LANES), BF),
        pltpu.VMEM((R, LANES), BF),
        pltpu.VMEM((R, LANES), BF),
        pltpu.VMEM((16, D), F32),
        pltpu.VMEM((stages + 1, 16, D), F32),
        pltpu.VMEM((10, D, FC), BF),
        *[pltpu.VMEM((2 * nf + 2, n, FC), BF) for n in rows_at],
        *[pltpu.VMEM((3 * pairs, n, LANES), BF) for n in rows_at],
        dma((2 * nf + 2, stages)), dma((2 * nf + 2, stages)),
        dma((3 * pairs, stages)), dma((3 * pairs, stages)),
        dma((15,)), dma((15,)), dma((stages + 1,)), dma((stages + 1,)), dma((14,)),
    ]
    mixed, grad_tokens, shard, small = pl.pallas_call(
        functools.partial(kernel, dp),
        out_shape=(
            jax.ShapeDtypeStruct((T, D), BF),
            jax.ShapeDtypeStruct((T, D), F32),
            jax.ShapeDtypeStruct((D // dp, columns), F32),
            jax.ShapeDtypeStruct((16, D), F32),
        ),
        in_specs=[hbm] * 6 + [smem] + [vmem] * 9,
        out_specs=(hbm, hbm, vmem, vmem),
        scratch_shapes=scratch,
        compiler_params=pltpu.CompilerParams(
            collective_id=0, has_side_effects=True, vmem_limit_bytes=63 << 20
        ),
        name="block",
    )(
        tokens, cotangent, proj_weight, out_weight, up_weight, down_weight, episode_lengths,
        row(attn_gain), row(attn_shift), row(proj_bias), row(out_bias), row(mlp_gain), row(mlp_shift),
        row(up_bias), row(down_bias), jnp.asarray(rope_tables()),
    )
    down = shard[:, :F].T
    up = shard[:, F : 2 * F]
    out = shard[:, 2 * F : 2 * F + E].T
    proj = jnp.stack([shard[:, 2 * F + (1 + c) * E : 2 * F + (2 + c) * E] for c in range(3)])
    return (
        mixed, grad_tokens, small[0], small[1], proj, small[2:5], out, small[5], small[6], small[7],
        up, small[8:12].reshape(-1), down, small[12],
    )


def solution(mesh):
    rows = P(("dp", "tensor"), None)
    return jax.shard_map(
        on_device,
        mesh=mesh,
        in_specs=(
            rows, P("dp", None), P(), P(), P(None, None, "tensor"), P(None, "tensor"), P("tensor", None), P(),
            P(), P(), P(None, "tensor"), P("tensor"), P("tensor", None), P(), rows,
        ),
        out_specs=(
            rows, rows, P(), P(), P(None, "dp", "tensor"), P(), P("tensor", "dp"), P(), P(), P(),
            P("dp", "tensor"), P(), P("tensor", "dp"), P(),
        ),
        check_vma=False,
    )
```

```python
import functools
import math

import jax
import jax.numpy as jnp
import ml_dtypes
import numpy as np
from jax import lax
from jax.experimental import pallas as pl
from jax.experimental.pallas import tpu as pltpu
from jax.sharding import PartitionSpec as P

HEAD = 64
GRID = 16
FRAME = 258
EPS = 1e-6
LANES = 128
FC = 256
MESH = pl.DeviceIdType.MESH
F32 = jnp.float32
BF = jnp.bfloat16
NEG = -1e30
FRAMES = 4
TERM = 16


def nn(a, b):
    return jnp.dot(a, b, preferred_element_type=F32)


def nt(a, b):
    return lax.dot_general(a, b, (((1,), (1,)), ((), ())), preferred_element_type=F32)


def rope_tables():
    side = 2 * (HEAD // 6)
    sections = (HEAD - 2 * side, side, side)
    cos = np.zeros((FRAMES + 2 * GRID, HEAD), np.float64)
    sin = np.zeros((FRAMES + 2 * GRID, HEAD), np.float64)
    lane, row = 0, 0
    for width, count in zip(sections, (FRAMES, GRID, GRID)):
        half = width // 2
        freq = np.float32(10000.0) ** (-np.arange(half, dtype=np.float32) * np.float32(2.0) / np.float32(width))
        angle = (np.arange(count, dtype=np.float32)[:, None] * freq.astype(np.float32)[None, :]).astype(np.float64)
        cos[row : row + count, lane : lane + half] = np.cos(angle)
        cos[row : row + count, lane + half : lane + width] = np.cos(angle)
        sin[row : row + count, lane : lane + half] = -np.sin(angle)
        sin[row : row + count, lane + half : lane + width] = np.sin(angle)
        lane, row = lane + width, row + count
    both = np.concatenate([cos, cos, sin, sin], axis=1).astype(np.float32)
    out = np.zeros((LANES, 4 * HEAD), ml_dtypes.bfloat16)
    rest, n = both, both.shape[0]
    for term in range(3):
        part = rest.astype(ml_dtypes.bfloat16)
        out[term * n : (term + 1) * n] = part
        rest = rest - part.astype(np.float32)
    return out


def partner_of(x, lane):
    side = 2 * (HEAD // 6)
    first = HEAD - 2 * side
    a, b = first // 2, side // 2
    within = lane % HEAD
    past = (within - first) % side
    up_a = pltpu.roll(x, LANES - a, 1)
    down_a = pltpu.roll(x, a, 1)
    up_b = pltpu.roll(x, LANES - b, 1)
    down_b = pltpu.roll(x, b, 1)
    in_first = jnp.where(within < a, up_a, down_a)
    in_side = jnp.where(past < b, up_b, down_b)
    return jnp.where(within < first, in_first, in_side)


def split3(x):
    hi = x.astype(BF).astype(F32)
    mid = (x - hi).astype(BF).astype(F32)
    return hi, mid, x - hi - mid


def kernel(
    dp, tok_h, cot_h, pw_h, ow_h, uw_h, dw_h, lens, gain1, shift1, pbias, obias, gain2, shift2, ubias, dbias, table,
    mixed_h, gtok_h, g_down, g_up, g_out, g_proj, small, U, DN, OW, TOKX, N1, T1, T2, CG, N2, QA, K, V, ATT, ACT, GH, MID, X1, S1,
    ONE, QF, KF, SB, SBR, WIDE, G, *rest,
):
    stages = dp.bit_length() - 1
    RM, RP = rest[:stages], rest[stages : 2 * stages]
    m_send, m_recv, p_send, p_recv, x_send, x_recv, b_send, b_recv, loads = rest[2 * stages :]
    T = tok_h.shape[0]
    D = tok_h.shape[1]
    R = 2 * T
    E = OW.shape[0]
    F = DN.shape[0]
    pairs = E // LANES
    nf = F // FC
    low = stages - 4
    unit = 1 << low
    me = lax.axis_index("dp")
    core = lax.axis_index("tensor")
    lane = lax.broadcasted_iota(jnp.int32, (1, LANES), 1)

    def bit_of(stride):
        return (me // stride) % 2

    def partner(stride):
        return me + (1 - 2 * bit_of(stride)) * stride

    def load(src, dst, k):
        return pltpu.make_async_copy(src, dst, loads.at[k])

    tok_load = load(tok_h, TOKX, 0)
    cot_load = load(cot_h, CG.at[pl.ds(0, T)], 1)
    ow_load = load(ow_h, OW, 2)
    uw_load = load(uw_h, U, 3)
    dw_load = load(dw_h, DN, 4)
    tok_again = load(tok_h, N2.at[pl.ds(0, T)], 5)
    mixed_store = load(N2.at[pl.ds(0, T)], mixed_h, 6)

    def projection_loads(k):
        return [
            load(
                pw_h.at[c, :, pl.ds(p * LANES, LANES)], U.at[:, pl.ds((3 * p + c) * LANES, LANES)],
                k + 3 * p + c,
            )
            for p in range(pairs)
            for c in range(3)
        ]

    pw_loads = projection_loads(8)
    pw_again = projection_loads(8 + 3 * pairs)

    def gtok_store(m):
        rows = pl.ds(m * (T // 2), T // 2)
        return load(WIDE.at[m], gtok_h.at[rows], 8 + 6 * pairs + m)

    tok_load.start()
    for c in pw_loads:
        c.start()
    cot_load.start()
    ow_load.start()
    dw_load.start()

    barrier = pltpu.get_barrier_semaphore()
    peers = [(partner(1 << b), core) for b in range(stages)] + [(me, 1 - core)]
    for who in peers:
        pl.semaphore_signal(barrier, inc=1, device_id=who, device_id_type=MESH)

    @pl.loop(0, R // 256)
    def _(m):
        row = lax.broadcasted_iota(jnp.int32, (256, 1), 0) + m * 256
        place = row + core * T
        place = jnp.where(place >= R, place - R, place)
        begin = jnp.zeros((256, 1), jnp.int32)
        episode = jnp.zeros((256, 1), jnp.int32)
        end = jnp.int32(0)
        for e in range(lens.shape[1] - 1):
            end = end + lens[0, e]
            begin = jnp.where(place >= end, end, begin)
            episode = jnp.where(place >= end, e + 1, episode)
        local = place - begin
        frame = jnp.zeros((256, 1), jnp.int32)
        for k in range(1, FRAMES):
            frame = jnp.where(local >= k * FRAME, k, frame)
        inside = local - frame * FRAME
        patch = jnp.maximum(inside - 2, 0)
        row_pos = jnp.where(inside >= 2, patch // GRID, 0)
        col_pos = jnp.where(inside >= 2, patch % GRID, 0)
        n = FRAMES + 2 * GRID
        spot = lane % n
        hit = (spot == frame) | (spot == FRAMES + row_pos) | (spot == FRAMES + GRID + col_pos)
        hit = hit & (lane < 3 * n)
        rows = pl.ds(m * 256, 256)
        ONE[rows] = jnp.where(hit, 1.0, 0.0).astype(BF)
        feature = lane % HEAD
        counted = (feature // FRAMES == episode) & (feature % FRAMES <= frame)
        is_class = feature < TERM
        QF[rows] = jnp.where(is_class & jnp.logical_not(counted), NEG, 0.0).astype(BF)
        ones = (feature == episode * FRAMES + frame) | ((feature >= TERM) & (feature < TERM + 3))
        KF[rows] = jnp.where(ones, 1.0, 0.0).astype(BF)

    def cross(src, dst, k):
        return pltpu.make_async_remote_copy(
            src_ref=src, dst_ref=dst, send_sem=x_send.at[k], recv_sem=x_recv.at[k],
            device_id=(me, 1 - core), device_id_type=MESH,
        )

    half = T // 2

    def turned(dst, src, first, count):
        @pl.loop(first // 256, (first + count) // 256)
        def _(m):
            rows = pl.ds(pl.multiple_of(m * 256, 256), 256)
            dst[:, rows] = src[rows].T

    def cross_rows(src, s0, dst, d0, base, m):
        return cross(src.at[pl.ds(s0 + m * half, half)], dst.at[pl.ds(d0 + m * half, half)], base + m)

    def order_of(kind, par):
        where = {"x": unit * (1 + par), "y": unit * (2 - par), "z": unit * 4, "Z": unit * 8}
        return [where[k] for k in kind + "Z"] + [1 << b for b in reversed(range(low))]

    def places_of(kind, par):
        w = {k: 8 >> i for i, k in enumerate(kind + "Z")}
        return (w["x"] + par * (w["y"] - w["x"]), w["y"] + par * (w["x"] - w["y"]), w["z"], w["Z"])

    def g_view(fam, c):
        if fam == "M":
            return G.at[(2 * c[0] + c[1]) % 8]
        if fam == "O":
            return G.at[2 + c]
        p, k = c
        return G.at[p + 4 * (k // 2), :, pl.ds((k % 2) * LANES, LANES)]

    def slot(fam, c):
        if fam == "M":
            return RM, 2 * c[0] + c[1], m_send, m_recv
        if fam == "O":
            return RM, 2 * nf + c, m_send, m_recv
        return RP, 3 * c[0] + c[1], p_send, p_recv

    block = D // 16

    def put(fam, c, value, row0, kind, par):
        w = places_of(kind, par)
        view = g_view(fam, c)
        for b in range(value.shape[0] // block):
            n = row0 * (value.shape[0] // block) + b
            place = ((n % 2) * w[0] + ((n // 2) % 2) * w[1] + ((n // 4) % 2) * w[2] + (n // 8) * w[3]) * block
            view[pl.ds(pl.multiple_of(place, block), block), :] = value[b * block : (b + 1) * block].astype(BF)

    def rs_parts(fam, c, s, order):
        R_, at, ss, rr = slot(fam, c)
        view = g_view(fam, c) if s == 0 else R_[s - 1].at[at]
        n = D >> s
        h = n // 2
        bit = bit_of(order[s])
        if h >= 16:
            src = view.at[pl.ds(pl.multiple_of((1 - bit) * h, 16), h)]
            keep = view.at[pl.ds(pl.multiple_of(bit * h, 16), h)]
        else:
            src = keep = view
        copy = pltpu.make_async_remote_copy(
            src_ref=src, dst_ref=R_[s].at[at], send_sem=ss.at[at, s], recv_sem=rr.at[at, s],
            device_id=(partner(order[s]), core), device_id_type=MESH,
        )
        return copy, keep, R_[s].at[at], bit, h

    def finish(fam, c, total):
        if fam == "M":
            into = g_down if c[1] == 0 else g_up
            into[:, pl.ds(pl.multiple_of(c[0] * FC, FC), FC)] = total
        elif fam == "O":
            g_out[:, c * FC : (c + 1) * FC] = total
        else:
            g_proj[c[1], :, pl.ds(pl.multiple_of(c[0] * LANES, LANES), LANES)] = total

    def rs_start(fam, c, s, order):
        rs_parts(fam, c, s, order)[0].start()

    def rs_step(fam, c, s, order):
        copy, keep, landed, bit, h = rs_parts(fam, c, s, order)
        copy.wait()
        if s < stages - 1:
            n = landed.shape[0]
            piece = min(n, 64)
            if n == piece:
                landed[...] = landed[...] + keep[...]
            else:
                @pl.loop(0, n // piece)
                def _(q):
                    at = pl.ds(pl.multiple_of(q * piece, piece), piece)
                    landed[at] = landed[at] + keep[at]

            rs_start(fam, c, s + 1, order)
        else:
            total = landed[...].astype(F32) + keep[...].astype(F32)
            if h < 16:
                total = jnp.where(bit == 1, total[8:], total[:8])
            finish(fam, c, total)

    plan = make_plan(stages, nf, pairs)

    def poll(point, at=None):
        if at is None:
            for fam, c, s in plan.pop((point, 0), ()):
                rs_step(fam, c, s, order_of(*kind_of(fam, c)))
            return
        for k in sorted(k for p, k in plan if p == point):
            @pl.when(at == k)
            def _():
                for fam, c, s in plan.pop((point, k)):
                    rs_step(fam, c, s, order_of(*kind_of(fam, c)))

    def normed(x):
        centre = x - jnp.mean(x, axis=1, keepdims=True)
        inv = lax.rsqrt(jnp.mean(centre * centre, axis=1, keepdims=True) + EPS)
        return centre * inv, inv

    tok_load.wait()

    @pl.loop(0, 2)
    def _(m):
        @pl.loop(0, half // 128)
        def _(q):
            rows = pl.ds(m * half + q * 128, 128)
            x = TOKX[rows].astype(F32)
            N1[rows] = (normed(x)[0] * gain1[...] + shift1[...]).astype(BF)

    def rotary(rows):
        both = nn(ONE[rows], table[...])
        return both[:, :LANES], both[:, LANES:]

    for c in pw_loads:
        c.wait()

    def project(m):
        rows = pl.ds(m * 256, 256)
        x = N1[rows]
        cos, sin = rotary(rows)
        all_three = nn(x, U[:, : 3 * E])
        for p in range(pairs):
            q, k, v = (
                all_three[:, (3 * p + c) * LANES : (3 * p + c + 1) * LANES]
                + pbias[c : c + 1, p * LANES : (p + 1) * LANES]
                for c in range(3)
            )
            q = ((q * cos + partner_of(q, lane) * sin) * HEAD**-0.5).astype(BF)
            QA[2 * p, rows] = jnp.where(lane < HEAD, q, QF[rows])
            QA[2 * p + 1, rows] = jnp.where(lane >= HEAD, q, QF[rows])
            K[rows, p * LANES : (p + 1) * LANES] = (k * cos + partner_of(k, lane) * sin).astype(BF)
            V[rows, p * LANES : (p + 1) * LANES] = v.astype(BF)

    @pl.loop(0, 2)
    def _(m):
        project(m)

    cot_load.wait()
    pl.semaphore_wait(barrier, len(peers))

    @pl.loop(0, 2)
    def _(m):
        cross_rows(N1, 0, N1, T, 1, m).start()

    cot_send = cross(CG.at[pl.ds(0, T)], CG.at[pl.ds(T, T)], 0)
    cot_send.start()
    turned(T1, CG, 0, T)

    @pl.loop(0, 2)
    def _(m):
        cross_rows(N1, 0, N1, T, 1, m).wait()
        project(2 + m)

    uw_load.start()

    def mine(e):
        return lane < HEAD if e == 0 else lane >= HEAD

    def key_sets(p, box):
        cols = pl.ds(pl.multiple_of(p * LANES, LANES), LANES)
        for e in range(2):
            box[:, e * LANES : (e + 1) * LANES] = jnp.where(mine(e), K[:, cols], KF[...])
            box[:, (2 + e) * LANES : (3 + e) * LANES] = jnp.where(mine(e), V[:, cols], jnp.ones((), BF))

    def attend(first):
        @pl.loop(0, pairs)
        def _(p):
            key_sets(p, T2)

            @pl.loop(0, T // 256, unroll=2)
            def _(b):
                rows = pl.ds(first + b * 256, 256)
                parts = []
                for e in range(2):
                    qa = QA[2 * p + e, rows]
                    s = nt(qa, T2[:, e * LANES : (e + 1) * LANES])
                    top = jnp.max(s, axis=1, keepdims=True)
                    w = jnp.exp(s - top).astype(BF)
                    o = nn(w, T2[:, (2 + e) * LANES : (3 + e) * LANES])
                    parts.append(o / pltpu.roll(o, HEAD, 1))
                    total = jnp.where(mine(e), 1.0, o)
                    hi, mid, lo = split3(top + jnp.log(total))
                    feature = lane % HEAD
                    terms = jnp.where(feature == TERM, -hi, jnp.where(feature == TERM + 1, -mid, -lo)).astype(BF)
                    is_term = (feature >= TERM) & (feature < TERM + 3) & jnp.logical_not(mine(e))
                    QA[2 * p + e, rows] = jnp.where(is_term, terms, qa)
                ATT[rows, pl.ds(pl.multiple_of(p * LANES, LANES), LANES)] = jnp.where(
                    lane < HEAD, parts[0], parts[1]
                ).astype(BF)

    attend(T)
    ow_load.wait()

    @pl.loop(0, 2)
    def _(m):
        rows = pl.ds(m * half, half)
        S1[rows] = nn(ATT[pl.ds(T + m * half, half)], OW[...]).astype(BF)
        cross_rows(S1, 0, X1, 0, 3, m).start()

    attend(0)

    @pl.loop(0, 2)
    def _(m):
        rows = pl.ds(m * half, half)
        MID[rows] = nn(ATT[rows], OW[...])
        cross_rows(S1, 0, X1, 0, 3, m).wait()

        @pl.loop(0, half // 128)
        def _(q):
            rows = pl.ds(m * half + q * 128, 128)
            mid = TOKX[rows].astype(F32) + (MID[rows] + X1[rows].astype(F32) + obias[...])
            MID[rows] = mid
            N2[rows] = (normed(mid)[0] * gain2[...] + shift2[...]).astype(BF)

        cross_rows(N2, 0, N2, T, 5, m).start()

    SB[...] = jnp.zeros_like(SB)
    SB[15:16] = jnp.sum(CG[0:T].astype(F32), axis=0, keepdims=True)
    turned(T2, N2, 0, T)
    cot_send.wait()
    turned(T1, CG, T, T)

    @pl.loop(0, 2)
    def _(m):
        cross_rows(N2, 0, N2, T, 5, m).wait()

    turned(T2, N2, T, T)
    uw_load.wait()
    dw_load.wait()

    ones8 = jnp.ones((8, R), BF)

    wide = 2 * FC

    @pl.loop(0, nf // 2)
    def _(j):
        cols = pl.ds(pl.multiple_of(j * wide, wide), wide)

        @pl.loop(0, R // 256)
        def _(m):
            rows = pl.ds(m * 256, 256)
            h = nn(N2[rows], U[:, cols]) + ubias[:, cols]
            cdf = 0.5 + 0.5 * lax.erf(h * math.sqrt(0.5))
            ACT[rows, cols] = (h * cdf).astype(BF)
            slope = cdf + h * jnp.exp(h * h * -0.5) * (1.0 / math.sqrt(2 * math.pi))
            GH[rows, cols] = (nt(CG[rows], DN[cols]) * slope).astype(BF)

        poll("hidden", j)
        for k, (left, right) in enumerate(((T1, ACT), (T2, GH))):
            @pl.loop(0, D // 512)
            def _(m):
                both = nn(left[pl.ds(m * 512, 512)], right[:, cols])
                for e in range(2):
                    put("M", (2 * j + e, k), both[:, e * FC : (e + 1) * FC], m, M_KINDS[2 * e + k], j % 2)

            for e in range(2):
                rs_start("M", (2 * j + e, k), 0, order_of(M_KINDS[2 * e + k], j % 2))
            poll("down" if k == 0 else "up", j)

        sums = nn(ones8, GH[:, cols])
        per = D // wide
        SB[pl.ds(11 + core * (F // D) + j // per, 1), pl.ds(pl.multiple_of((j % per) * wide, wide), wide)] = sums[0:1]
    tok_again.start()

    def norm_back(g, x, gain, row):
        xhat, inv = normed(x)
        SB[row : row + 1] += jnp.sum(g * xhat, axis=0, keepdims=True)
        SB[row + 1 : row + 2] += jnp.sum(g, axis=0, keepdims=True)
        gx = g * gain
        a = jnp.mean(gx, axis=1, keepdims=True)
        b = jnp.mean(gx * xhat, axis=1, keepdims=True)
        return inv * (gx - a - xhat * b)

    @pl.loop(0, 2)
    def _(m):
        S1[pl.ds(m * half, half)] = nt(GH[pl.ds(T + m * half, half)], U[...]).astype(BF)
        cross_rows(S1, 0, X1, 0, 7, m).start()

    poll("norm")

    @pl.loop(0, 2)
    def _(m):
        WIDE[0] = nt(GH[pl.ds(m * half, half)], U[...])
        cross_rows(S1, 0, X1, 0, 7, m).wait()

        @pl.loop(0, half // 64)
        def _(q):
            at = pl.ds(m * half + q * 64, 64)
            g = WIDE[0, pl.ds(q * 64, 64)] + X1[at].astype(F32)
            total = CG[at].astype(F32) + norm_back(g, MID[at], gain2[...], 9)
            high = total.astype(BF)
            CG[at] = high
            TOKX[at] = (total - high.astype(F32)).astype(BF)
            SB[8:9] += jnp.sum(high.astype(F32), axis=0, keepdims=True)

        cross_rows(CG, 0, CG, T, 9, m).start()
        poll("branch", m)

    for c in pw_again:
        c.start()

    def grad_attended(m):
        rows = pl.ds(m * half, half)
        GH[rows, 0:E] = nt(CG[rows], OW[...]).astype(BF)

    @pl.loop(0, 2)
    def _(m):
        grad_attended(m)

    turned(T1, CG, 0, T)
    poll("attended")

    @pl.loop(0, 2)
    def _(m):
        cross_rows(CG, 0, CG, T, 9, m).wait()
        grad_attended(2 + m)

    turned(T1, CG, T, T)

    @pl.loop(0, D // 512)
    def _(m):
        both = nn(T1[pl.ds(m * 512, 512)], ATT[...])
        for c in range(2):
            put("O", c, both[:, c * FC : (c + 1) * FC], m, O_KINDS[c], 0)

    for c in range(2):
        rs_start("O", c, 0, order_of(O_KINDS[c], 0))
    turned(T2, N1, 0, R)
    poll("out")

    def sums(g, s):
        who = (partner(1 << s), core) if s < stages else (me, 1 - core)
        return pltpu.make_async_remote_copy(
            src_ref=SB.at[pl.ds(8 * g, 8)], dst_ref=SBR.at[g, s],
            send_sem=b_send.at[g, s], recv_sem=b_recv.at[g, s],
            device_id=who, device_id_type=MESH,
        )

    def sum_start(g, s):
        sums(g, s).start()

    def sum_step(g, s):
        sums(g, s).wait()
        SB[8 * g : 8 * g + 8] = SB[8 * g : 8 * g + 8] + SBR[g, s]
        if s < stages:
            sum_start(g, s + 1)

    def key_grads(b, k):
        return pl.ds(pl.multiple_of((2 * b + k) * LANES, LANES), LANES)

    sum_start(1, 0)
    @pl.loop(0, pairs)
    def _(p):
        cols = pl.ds(pl.multiple_of(p * LANES, LANES), LANES)
        key_sets(p, T1)
        N1[0:LANES] = K[:, cols].T
        for e in range(2):
            @pl.loop(0, R // 256)
            def _(b):
                rows = pl.ds(b * 256, 256)
                g = GH[rows, cols]
                both = g.astype(F32) * ATT[rows, cols].astype(F32)
                inner = jnp.sum(jnp.where(mine(e), both, 0.0), axis=1, keepdims=True)
                hi, mid, lo = split3(inner)
                feature = lane % HEAD
                terms = jnp.where(feature == TERM, -hi, jnp.where(feature == TERM + 1, -mid, -lo))
                is_term = (feature >= TERM) & (feature < TERM + 3)
                terms = jnp.where(is_term, terms, 0.0).astype(BF)
                T1[rows, (4 + e) * LANES : (5 + e) * LANES] = jnp.where(mine(e), g, terms)

        for e in range(2):
            WIDE[1, e * HEAD : (e + 1) * HEAD] = jnp.zeros((HEAD, R), F32)

        poll("keys", p)

        @pl.loop(0, R // 256)
        def _(b):
            rows = pl.ds(b * 256, 256)
            pair = []
            for e in range(2):
                dk = dv = 0.0
                for a in range(2):
                    across = pl.ds(a * T, T)
                    qa = QA[2 * p + e, across]
                    ga = T1[across, (4 + e) * LANES : (5 + e) * LANES]
                    w = jnp.exp(nt(T1[rows, e * LANES : (e + 1) * LANES], qa))
                    ds = (w * nt(T1[rows, (2 + e) * LANES : (3 + e) * LANES], ga)).astype(BF)
                    dv += nn(w.astype(BF), ga)
                    dk += nn(ds, qa)
                    WIDE[1, e * HEAD : (e + 1) * HEAD, across] += nn(N1[e * HEAD : (e + 1) * HEAD, rows], ds)
                pair.append((dk, dv))
            for k, (g0, g1) in enumerate(zip(*pair)):
                WIDE[0, :, key_grads(b, k)] = jnp.where(mine(0), g0, g1)
            poll("inner", p * (R // 256) + b)

        @pl.loop(0, R // 256)
        def _(b):
            rows = pl.ds(b * 256, 256)
            cos, sin = rotary(rows)

            def back(g):
                g = g.astype(BF).astype(F32)
                return g * cos - partner_of(g, lane) * sin

            parts = (
                back(WIDE[1, 0:LANES, rows].T) * HEAD**-0.5,
                back(WIDE[0, :, key_grads(b, 0)]),
                WIDE[0, :, key_grads(b, 1)],
            )
            for c, part in enumerate(parts):
                GH[rows, pl.ds(pl.multiple_of(E + (3 * p + c) * LANES, LANES), LANES)] = part.astype(BF)

        own_cols = pl.ds(pl.multiple_of(E + 3 * p * LANES, LANES), 3 * LANES)

        @pl.loop(0, D // 512)
        def _(m):
            three = nn(T2[pl.ds(m * 512, 512)], GH[:, own_cols])
            for c in range(3):
                put("P", (p, c), three[:, c * LANES : (c + 1) * LANES], m, P_KINDS[c], 0)

        for c in range(3):
            rs_start("P", (p, c), 0, order_of(P_KINDS[c], 0))
        totals = nn(ones8, GH[:, own_cols])[0:1]
        for c in range(3):
            at = pl.multiple_of(core * E + p * LANES, LANES)
            SB[2 + c : 3 + c, pl.ds(at, LANES)] = totals[:, c * LANES : (c + 1) * LANES]

        poll("pair", p)
        for q in range(min(pairs, stages + 1)):
            @pl.when(p == q)
            def _():
                sum_step(1, q)

    for c in pw_again:
        c.wait()

    @pl.loop(0, 2)
    def _(m):
        S1[pl.ds(m * half, half)] = nt(GH[pl.ds(T + m * half, half), E : 4 * E], U[:, : 3 * E]).astype(BF)
        cross_rows(S1, 0, X1, 0, 13, m).start()

    poll("input")
    tok_again.wait()

    @pl.loop(0, 2)
    def _(m):
        rows = pl.ds(m * half, half)
        WIDE[m] = nt(GH[rows, E : 4 * E], U[:, : 3 * E])
        cross_rows(S1, 0, X1, 0, 13, m).wait()

        @pl.loop(0, half // 64)
        def _(q):
            at = pl.ds(m * half + q * 64, 64)
            here = pl.ds(q * 64, 64)
            g = WIDE[m, here] + X1[at].astype(F32)
            before = CG[at].astype(F32) + TOKX[at].astype(F32)
            WIDE[m, here] = before + norm_back(g, N2[at].astype(F32), gain1[...], 0)


        gtok_store(m).start()

    sum_start(0, 0)

    poll("tokens")

    @pl.loop(0, 2)
    def _(m):
        S1[pl.ds(m * half, half)] = nn(ACT[pl.ds(T + m * half, half)], DN[...]).astype(BF)
        cross_rows(S1, 0, N2, T, 11, m).start()

    early = list(range(pairs, stages + 1))
    if early:
        sum_step(1, early.pop(0))
    sum_step(0, 0)
    poll("mixed")

    @pl.loop(0, 2)
    def _(m):
        rows = pl.ds(m * half, half)
        MID[rows] += nn(ACT[rows], DN[...])
        cross_rows(S1, 0, N2, T, 11, m).wait()

        @pl.loop(0, half // 64)
        def _(q):
            at = pl.ds(m * half + q * 64, 64)
            other = N2[pl.ds(T + m * half + q * 64, 64)].astype(F32)
            N2[at] = (MID[at] + (other + dbias[...])).astype(BF)

    mixed_store.start()
    for s in range(1, stages + 1):
        if early:
            sum_step(1, early.pop(0))
        sum_step(0, s)
        poll("last%d" % s)
    poll("rest")
    assert not plan
    small[...] = SB[...]
    mixed_store.wait()
    for m in range(2):
        gtok_store(m).wait()


def hand_over(*refs):
    arrive = [pltpu.make_async_copy(refs[k], refs[-8 + k], refs[-2].at[k]) for k in range(6)]
    leave = [pltpu.make_async_copy(refs[-8 + k], refs[7 + k], refs[-1].at[k]) for k in range(6)]
    for c in arrive:
        c.start()
    small, vectors = refs[6], refs[13:21]
    for v, at in zip(vectors, (0, 1, 8, 9, 10, 15)):
        v[...] = small[at : at + 1]
    vectors[6][...] = small[2:5]
    vectors[7][...] = small[11:15]
    for k in range(6):
        arrive[k].wait()
        leave[k].start()
    for c in leave:
        c.wait()


M_KINDS = ("xyz", "yzx", "zxy", "yxz")
O_KINDS = ("xzy", "zyx")
P_KINDS = ("xyz", "yzx", "zxy")


def kind_of(fam, c):
    if fam == "M":
        return M_KINDS[2 * (c[0] % 2) + c[1]], (c[0] // 2) % 2
    if fam == "O":
        return O_KINDS[c], 0
    return P_KINDS[c[1]], 0


def make_plan(stages, nf, pairs):
    now, free, flying, plan = 0.0, {}, {}, {}

    def send(fam, c, s):
        kind, par = kind_of(fam, c)
        axes = [a if not par or a == "z" else "yx"["xy".index(a)] for a in kind] + ["z"] + ["w"] * stages
        size = (FC if fam != "P" else LANES) / FC * WIRE / 2**s
        begin = max(now, free.get(axes[s], 0.0))
        free[axes[s]] = begin + size
        flying[(fam, c, s)] = begin + size + LATENCY

    def take(point, at, only=None, everything=False):
        nonlocal now
        while True:
            ready = [
                (t, k) for k, t in flying.items()
                if (everything or t <= now + SLACK or (only and only(k))) and (only is None or only(k))
            ]
            if not ready:
                return
            t, k = min(ready)
            del flying[k]
            now = max(now, t) + STEP
            plan.setdefault((point, at), []).append(k)
            if k[2] < stages - 1:
                send(k[0], k[1], k[2] + 1)

    def first(k):
        return k[0] == "M" and k[2] == 0

    for j in range(nf // 2):
        now += TIMES["hidden"]
        take("hidden", j, lambda k: first(k) and k[1][0] // 2 <= j - 2)
        take("hidden", j)
        for k, point in enumerate(("down", "up")):
            now += TIMES[point]
            for e in range(2):
                send("M", (2 * j + e, k), 0)
            take(point, j)
    now += TIMES["norm"]
    take("norm", 0)
    for m in range(2):
        now += TIMES["branch"]
        take("branch", m)
    now += TIMES["attended"]
    take("attended", 0, lambda k: first(k) and k[1][0] == nf - 3)
    take("attended", 0)
    now += TIMES["out"]
    for c in range(2):
        send("O", c, 0)
    take("out", 0)
    for p in range(pairs):
        now += TIMES["keys"]
        if p == 0:
            take("keys", p, first)
        if p == 2:
            take("keys", p, lambda k: k[0] == "O" and k[2] == 0)
        take("keys", p)
        for b in range(4):
            now += TIMES["inner"]
            take("inner", 4 * p + b)
        now += TIMES["pair"]
        for c in range(3):
            send("P", (p, c), 0)
        take("pair", p)
    for point in ("input", "tokens", "mixed"):
        now += TIMES[point]
        take(point, 0)
    now += TIMES["last"]
    for s in range(1, stages + 1):
        now += 2.0
        take("last%d" % s, 0)
    take("rest", 0, everything=True)
    return plan


WIRE = 8.0
LATENCY = 6.0
SLACK = 0.0
STEP = 0.3
TIMES = dict(
    hidden=3.0, down=1.5, up=1.6, norm=2.6, branch=2.5, attended=1.8, out=4.0, keys=2.4, inner=1.7,
    pair=3.0, input=1.8, tokens=4.0, mixed=2.6, last=3.0,
)


def on_device(
    tokens, episode_lengths, attn_gain, attn_shift, proj_weight, proj_bias, out_weight, out_bias,
    mlp_gain, mlp_shift, up_weight, up_bias, down_weight, down_bias, cotangent,
):
    dp = lax.axis_size("dp")
    stages = dp.bit_length() - 1
    T, D = tokens.shape
    R = 2 * T
    E = proj_weight.shape[2]
    F = up_weight.shape[1]
    pairs = E // LANES
    nf = F // FC
    row = lambda v: v.reshape(1, -1).astype(F32)
    rows_at = [max(D >> (s + 1), 16) for s in range(stages)]
    vmem = pl.BlockSpec(memory_space=pltpu.VMEM)
    hbm = pl.BlockSpec(memory_space=pl.ANY)
    smem = pl.BlockSpec(memory_space=pltpu.SMEM)
    dma = pltpu.SemaphoreType.DMA
    scratch = [
        pltpu.VMEM((D, F), BF),
        pltpu.VMEM((F, D), BF),
        pltpu.VMEM((E, D), BF),
        pltpu.VMEM((T, D), BF),
        pltpu.VMEM((R, D), BF),
        pltpu.VMEM((D, R), BF),
        pltpu.VMEM((D, R), BF),
        pltpu.VMEM((R, D), BF),
        pltpu.VMEM((R, D), BF),
        pltpu.VMEM((2 * pairs, R, LANES), BF),
        pltpu.VMEM((R, E), BF),
        pltpu.VMEM((R, E), BF),
        pltpu.VMEM((R, E), BF),
        pltpu.VMEM((R, F), BF),
        pltpu.VMEM((R, F), BF),
        pltpu.VMEM((T, D), F32),
        pltpu.VMEM((T, D), BF),
        pltpu.VMEM((T, D), BF),
        pltpu.VMEM((R, LANES), BF),
        pltpu.VMEM((R, LANES), BF),
        pltpu.VMEM((R, LANES), BF),
        pltpu.VMEM((16, D), F32),
        pltpu.VMEM((2, stages + 1, 8, D), F32),
        pltpu.VMEM((2, T // 2, D), F32),
        pltpu.VMEM((8, D, FC), BF),
        *[pltpu.VMEM((2 * nf + 2, n, FC), BF) for n in rows_at],
        *[pltpu.VMEM((3 * pairs, n, LANES), BF) for n in rows_at],
        dma((2 * nf + 2, stages)), dma((2 * nf + 2, stages)),
        dma((3 * pairs, stages)), dma((3 * pairs, stages)),
        dma((15,)), dma((15,)), dma((2, stages + 1)), dma((2, stages + 1)), dma((10 + 6 * pairs,)),
    ]
    n = D // dp
    struct = jax.ShapeDtypeStruct
    made = pl.pallas_call(
        functools.partial(kernel, dp),
        out_shape=(
            struct((T, D), BF), struct((T, D), F32), struct((n, F), F32), struct((n, F), F32),
            struct((n, E), F32), struct((3, n, E), F32), struct((16, D), F32),
        ),
        in_specs=[hbm] * 6 + [smem] + [vmem] * 9,
        out_specs=(hbm, hbm, vmem, vmem, vmem, vmem, vmem),
        scratch_shapes=scratch,
        compiler_params=pltpu.CompilerParams(
            collective_id=0, has_side_effects=True, vmem_limit_bytes=63 << 20
        ),
        name="block",
    )(
        tokens, cotangent, proj_weight, out_weight, up_weight, down_weight, episode_lengths,
        row(attn_gain), row(attn_shift), proj_bias, row(out_bias), row(mlp_gain), row(mlp_shift),
        row(up_bias), row(down_bias), jnp.asarray(rope_tables()),
    )
    vectors = [struct((1, D), F32)] * 6 + [struct((3, D), F32), struct((4, D), F32)]
    mixed, grad_tokens, down, up, out, proj, gain1, shift1, obias, gain2, shift2, dbias, pbias, ubias = pl.pallas_call(
        hand_over,
        out_shape=tuple(struct(v.shape, v.dtype) for v in made[:6]) + tuple(vectors),
        in_specs=[hbm] * 6 + [vmem],
        out_specs=(hbm,) * 6 + (vmem,) * 8,
        scratch_shapes=[*(pltpu.VMEM(v.shape, v.dtype) for v in made[:6]), dma((6,)), dma((6,))],
        name="outputs",
    )(*made)
    return (
        mixed, grad_tokens, gain1[0], shift1[0], proj, pbias, out.T, obias[0], gain2[0], shift2[0],
        up, ubias.reshape(-1), down.T, dbias[0],
    )


def solution(mesh):
    rows = P(("dp", "tensor"), None)
    return jax.shard_map(
        on_device,
        mesh=mesh,
        in_specs=(
            rows, P("dp", None), P(), P(), P(None, None, "tensor"), P(None, "tensor"), P("tensor", None), P(),
            P(), P(), P(None, "tensor"), P("tensor"), P("tensor", None), P(), rows,
        ),
        out_specs=(
            rows, rows, P(), P(), P(None, "dp", "tensor"), P(), P("tensor", "dp"), P(), P(), P(),
            P("dp", "tensor"), P(), P("tensor", "dp"), P(),
        ),
        check_vma=False,
    )
```

```python
import functools
import math

import jax
import jax.numpy as jnp
import ml_dtypes
import numpy as np
from jax import lax
from jax.experimental import pallas as pl
from jax.experimental.pallas import tpu as pltpu
from jax.sharding import PartitionSpec as P

HEAD = 64
GRID = 16
FRAME = 258
EPS = 1e-6
LANES = 128
FC = 256
MESH = pl.DeviceIdType.MESH
F32 = jnp.float32
BF = jnp.bfloat16
NEG = -1e30
FRAMES = 4
TERM = 16


def nn(a, b):
    return jnp.dot(a, b, preferred_element_type=F32)


def nt(a, b):
    return lax.dot_general(a, b, (((1,), (1,)), ((), ())), preferred_element_type=F32)


def rope_tables():
    side = 2 * (HEAD // 6)
    sections = (HEAD - 2 * side, side, side)
    cos = np.zeros((FRAMES + 2 * GRID, HEAD), np.float64)
    sin = np.zeros((FRAMES + 2 * GRID, HEAD), np.float64)
    lane, row = 0, 0
    for width, count in zip(sections, (FRAMES, GRID, GRID)):
        half = width // 2
        freq = np.float32(10000.0) ** (-np.arange(half, dtype=np.float32) * np.float32(2.0) / np.float32(width))
        angle = (np.arange(count, dtype=np.float32)[:, None] * freq.astype(np.float32)[None, :]).astype(np.float64)
        cos[row : row + count, lane : lane + half] = np.cos(angle)
        cos[row : row + count, lane + half : lane + width] = np.cos(angle)
        sin[row : row + count, lane : lane + half] = -np.sin(angle)
        sin[row : row + count, lane + half : lane + width] = np.sin(angle)
        lane, row = lane + width, row + count
    both = np.concatenate([cos, cos, sin, sin], axis=1).astype(np.float32)
    out = np.zeros((LANES, 4 * HEAD), ml_dtypes.bfloat16)
    rest, n = both, both.shape[0]
    for term in range(3):
        part = rest.astype(ml_dtypes.bfloat16)
        out[term * n : (term + 1) * n] = part
        rest = rest - part.astype(np.float32)
    return out


def partner_of(x, lane):
    side = 2 * (HEAD // 6)
    first = HEAD - 2 * side
    a, b = first // 2, side // 2
    within = lane % HEAD
    past = (within - first) % side
    up_a = pltpu.roll(x, LANES - a, 1)
    down_a = pltpu.roll(x, a, 1)
    up_b = pltpu.roll(x, LANES - b, 1)
    down_b = pltpu.roll(x, b, 1)
    in_first = jnp.where(within < a, up_a, down_a)
    in_side = jnp.where(past < b, up_b, down_b)
    return jnp.where(within < first, in_first, in_side)


def split3(x):
    hi = x.astype(BF).astype(F32)
    mid = (x - hi).astype(BF).astype(F32)
    return hi, mid, x - hi - mid


def kernel(
    dp, tok_h, cot_h, pw_h, ow_h, uw_h, dw_h, lens, gain1, shift1, pbias, obias, gain2, shift2, ubias, dbias, table,
    mixed_h, gtok_h, g_down, g_up, g_out, g_proj, small, U, DN, OW, TOKX, N1, T1, T2, CG, N2, QA, K, V, ATT, ACT, GH, MID, X1, S1,
    ONE, QF, KF, SB, SBR, WIDE, G, *rest,
):
    stages = dp.bit_length() - 1
    RM, RP = rest[:stages], rest[stages : 2 * stages]
    m_send, m_recv, p_send, p_recv, x_send, x_recv, b_send, b_recv, loads = rest[2 * stages :]
    T = tok_h.shape[0]
    D = tok_h.shape[1]
    R = 2 * T
    E = OW.shape[0]
    F = DN.shape[0]
    pairs = E // LANES
    nf = F // FC
    low = stages - 4
    unit = 1 << low
    me = lax.axis_index("dp")
    core = lax.axis_index("tensor")
    lane = lax.broadcasted_iota(jnp.int32, (1, LANES), 1)

    def bit_of(stride):
        return (me // stride) % 2

    def partner(stride):
        return me + (1 - 2 * bit_of(stride)) * stride

    def load(src, dst, k):
        return pltpu.make_async_copy(src, dst, loads.at[k])

    tok_load = load(tok_h, TOKX, 0)
    cot_load = load(cot_h, CG.at[pl.ds(0, T)], 1)
    ow_load = load(ow_h, OW, 2)
    uw_load = load(uw_h, U, 3)
    dw_load = load(dw_h, DN, 4)
    tok_again = load(tok_h, N2.at[pl.ds(0, T)], 5)
    mixed_store = load(N2.at[pl.ds(0, T)], mixed_h, 6)

    def projection_loads(k):
        return [
            load(
                pw_h.at[c, :, pl.ds(p * LANES, LANES)], U.at[:, pl.ds((3 * p + c) * LANES, LANES)],
                k + 3 * p + c,
            )
            for p in range(pairs)
            for c in range(3)
        ]

    pw_loads = projection_loads(8)
    pw_again = projection_loads(8 + 3 * pairs)

    def gtok_store(m):
        rows = pl.ds(m * (T // 2), T // 2)
        return load(WIDE.at[m], gtok_h.at[rows], 8 + 6 * pairs + m)

    tok_load.start()
    for c in pw_loads:
        c.start()
    cot_load.start()
    ow_load.start()
    dw_load.start()

    barrier = pltpu.get_barrier_semaphore()
    peers = [(partner(1 << b), core) for b in range(stages)] + [(me, 1 - core)]
    for who in peers:
        pl.semaphore_signal(barrier, inc=1, device_id=who, device_id_type=MESH)

    @pl.loop(0, R // 256)
    def _(m):
        row = lax.broadcasted_iota(jnp.int32, (256, 1), 0) + m * 256
        place = row + core * T
        place = jnp.where(place >= R, place - R, place)
        begin = jnp.zeros((256, 1), jnp.int32)
        episode = jnp.zeros((256, 1), jnp.int32)
        end = jnp.int32(0)
        for e in range(lens.shape[1] - 1):
            end = end + lens[0, e]
            begin = jnp.where(place >= end, end, begin)
            episode = jnp.where(place >= end, e + 1, episode)
        local = place - begin
        frame = jnp.zeros((256, 1), jnp.int32)
        for k in range(1, FRAMES):
            frame = jnp.where(local >= k * FRAME, k, frame)
        inside = local - frame * FRAME
        patch = jnp.maximum(inside - 2, 0)
        row_pos = jnp.where(inside >= 2, patch // GRID, 0)
        col_pos = jnp.where(inside >= 2, patch % GRID, 0)
        n = FRAMES + 2 * GRID
        spot = lane % n
        hit = (spot == frame) | (spot == FRAMES + row_pos) | (spot == FRAMES + GRID + col_pos)
        hit = hit & (lane < 3 * n)
        rows = pl.ds(m * 256, 256)
        ONE[rows] = jnp.where(hit, 1.0, 0.0).astype(BF)
        feature = lane % HEAD
        counted = (feature // FRAMES == episode) & (feature % FRAMES <= frame)
        is_class = feature < TERM
        QF[rows] = jnp.where(is_class & jnp.logical_not(counted), NEG, 0.0).astype(BF)
        ones = (feature == episode * FRAMES + frame) | ((feature >= TERM) & (feature < TERM + 3))
        KF[rows] = jnp.where(ones, 1.0, 0.0).astype(BF)

    def cross(src, dst, k):
        return pltpu.make_async_remote_copy(
            src_ref=src, dst_ref=dst, send_sem=x_send.at[k], recv_sem=x_recv.at[k],
            device_id=(me, 1 - core), device_id_type=MESH,
        )

    half = T // 2

    def turned(dst, src, first, count):
        @pl.loop(first // 256, (first + count) // 256)
        def _(m):
            rows = pl.ds(pl.multiple_of(m * 256, 256), 256)
            dst[:, rows] = src[rows].T

    def cross_rows(src, s0, dst, d0, base, m):
        return cross(src.at[pl.ds(s0 + m * half, half)], dst.at[pl.ds(d0 + m * half, half)], base + m)

    def order_of(kind, par):
        where = {"x": unit * (1 + par), "y": unit * (2 - par), "z": unit * 4, "Z": unit * 8}
        return [where[k] for k in kind + "Z"] + [1 << b for b in reversed(range(low))]

    def places_of(kind, par):
        w = {k: 8 >> i for i, k in enumerate(kind + "Z")}
        return (w["x"] + par * (w["y"] - w["x"]), w["y"] + par * (w["x"] - w["y"]), w["z"], w["Z"])

    def g_view(fam, c):
        if fam == "M":
            return G.at[(2 * c[0] + c[1]) % 8]
        if fam == "O":
            return G.at[2 + c]
        p, k = c
        return G.at[p + 4 * (k // 2), :, pl.ds((k % 2) * LANES, LANES)]

    def slot(fam, c):
        if fam == "M":
            return RM, 2 * c[0] + c[1], m_send, m_recv
        if fam == "O":
            return RM, 2 * nf + c, m_send, m_recv
        return RP, 3 * c[0] + c[1], p_send, p_recv

    block = D // 16

    def put(fam, c, value, row0, kind, par):
        w = places_of(kind, par)
        view = g_view(fam, c)
        for b in range(value.shape[0] // block):
            n = row0 * (value.shape[0] // block) + b
            place = ((n % 2) * w[0] + ((n // 2) % 2) * w[1] + ((n // 4) % 2) * w[2] + (n // 8) * w[3]) * block
            view[pl.ds(pl.multiple_of(place, block), block), :] = value[b * block : (b + 1) * block].astype(BF)

    def rs_parts(fam, c, s, order):
        R_, at, ss, rr = slot(fam, c)
        view = g_view(fam, c) if s == 0 else R_[s - 1].at[at]
        n = D >> s
        h = n // 2
        bit = bit_of(order[s])
        if h >= 16:
            src = view.at[pl.ds(pl.multiple_of((1 - bit) * h, 16), h)]
            keep = view.at[pl.ds(pl.multiple_of(bit * h, 16), h)]
        else:
            src = keep = view
        copy = pltpu.make_async_remote_copy(
            src_ref=src, dst_ref=R_[s].at[at], send_sem=ss.at[at, s], recv_sem=rr.at[at, s],
            device_id=(partner(order[s]), core), device_id_type=MESH,
        )
        return copy, keep, R_[s].at[at], bit, h

    def finish(fam, c, total):
        if fam == "M":
            into = g_down if c[1] == 0 else g_up
            into[:, pl.ds(pl.multiple_of(c[0] * FC, FC), FC)] = total
        elif fam == "O":
            g_out[:, c * FC : (c + 1) * FC] = total
        else:
            g_proj[c[1], :, pl.ds(pl.multiple_of(c[0] * LANES, LANES), LANES)] = total

    def rs_start(fam, c, s, order):
        rs_parts(fam, c, s, order)[0].start()

    def rs_step(fam, c, s, order):
        copy, keep, landed, bit, h = rs_parts(fam, c, s, order)
        copy.wait()
        if s < stages - 1:
            n = landed.shape[0]
            piece = min(n, 64)
            if n == piece:
                landed[...] = landed[...] + keep[...]
            else:
                @pl.loop(0, n // piece)
                def _(q):
                    at = pl.ds(pl.multiple_of(q * piece, piece), piece)
                    landed[at] = landed[at] + keep[at]

            rs_start(fam, c, s + 1, order)
        else:
            total = landed[...].astype(F32) + keep[...].astype(F32)
            if h < 16:
                total = jnp.where(bit == 1, total[8:], total[:8])
            finish(fam, c, total)

    plan = make_plan(stages, nf, pairs)

    def poll(point, at=None):
        if at is None:
            for fam, c, s in plan.pop((point, 0), ()):
                rs_step(fam, c, s, order_of(*kind_of(fam, c)))
            return
        for k in sorted(k for p, k in plan if p == point):
            @pl.when(at == k)
            def _():
                for fam, c, s in plan.pop((point, k)):
                    rs_step(fam, c, s, order_of(*kind_of(fam, c)))

    def normed(x):
        centre = x - jnp.mean(x, axis=1, keepdims=True)
        inv = lax.rsqrt(jnp.mean(centre * centre, axis=1, keepdims=True) + EPS)
        return centre * inv, inv

    tok_load.wait()

    @pl.loop(0, 2)
    def _(m):
        @pl.loop(0, half // 128)
        def _(q):
            rows = pl.ds(m * half + q * 128, 128)
            x = TOKX[rows].astype(F32)
            N1[rows] = (normed(x)[0] * gain1[...] + shift1[...]).astype(BF)

    def rotary(rows):
        both = nn(ONE[rows], table[...])
        return both[:, :LANES], both[:, LANES:]

    for c in pw_loads:
        c.wait()

    def project(m):
        rows = pl.ds(m * 256, 256)
        x = N1[rows]
        cos, sin = rotary(rows)
        all_three = nn(x, U[:, : 3 * E])
        for p in range(pairs):
            q, k, v = (
                all_three[:, (3 * p + c) * LANES : (3 * p + c + 1) * LANES]
                + pbias[c : c + 1, p * LANES : (p + 1) * LANES]
                for c in range(3)
            )
            q = ((q * cos + partner_of(q, lane) * sin) * HEAD**-0.5).astype(BF)
            QA[2 * p, rows] = jnp.where(lane < HEAD, q, QF[rows])
            QA[2 * p + 1, rows] = jnp.where(lane >= HEAD, q, QF[rows])
            K[rows, p * LANES : (p + 1) * LANES] = (k * cos + partner_of(k, lane) * sin).astype(BF)
            V[rows, p * LANES : (p + 1) * LANES] = v.astype(BF)

    @pl.loop(0, 2)
    def _(m):
        project(m)

    cot_load.wait()
    pl.semaphore_wait(barrier, len(peers))

    @pl.loop(0, 2)
    def _(m):
        cross_rows(N1, 0, N1, T, 1, m).start()

    cot_send = cross(CG.at[pl.ds(0, T)], CG.at[pl.ds(T, T)], 0)
    cot_send.start()
    turned(T1, CG, 0, T)

    @pl.loop(0, 2)
    def _(m):
        cross_rows(N1, 0, N1, T, 1, m).wait()
        project(2 + m)

    uw_load.start()

    def mine(e):
        return lane < HEAD if e == 0 else lane >= HEAD

    def key_sets(p, box):
        cols = pl.ds(pl.multiple_of(p * LANES, LANES), LANES)
        for e in range(2):
            box[:, e * LANES : (e + 1) * LANES] = jnp.where(mine(e), K[:, cols], KF[...])
            box[:, (2 + e) * LANES : (3 + e) * LANES] = jnp.where(mine(e), V[:, cols], jnp.ones((), BF))

    def attend(first):
        @pl.loop(0, pairs)
        def _(p):
            key_sets(p, T2)

            @pl.loop(0, T // 256, unroll=2)
            def _(b):
                rows = pl.ds(first + b * 256, 256)
                parts = []
                for e in range(2):
                    qa = QA[2 * p + e, rows]
                    s = nt(qa, T2[:, e * LANES : (e + 1) * LANES])
                    top = jnp.max(s, axis=1, keepdims=True)
                    w = jnp.exp(s - top).astype(BF)
                    o = nn(w, T2[:, (2 + e) * LANES : (3 + e) * LANES])
                    parts.append(o / pltpu.roll(o, HEAD, 1))
                    total = jnp.where(mine(e), 1.0, o)
                    hi, mid, lo = split3(top + jnp.log(total))
                    feature = lane % HEAD
                    terms = jnp.where(feature == TERM, -hi, jnp.where(feature == TERM + 1, -mid, -lo)).astype(BF)
                    is_term = (feature >= TERM) & (feature < TERM + 3) & jnp.logical_not(mine(e))
                    QA[2 * p + e, rows] = jnp.where(is_term, terms, qa)
                ATT[rows, pl.ds(pl.multiple_of(p * LANES, LANES), LANES)] = jnp.where(
                    lane < HEAD, parts[0], parts[1]
                ).astype(BF)

    attend(T)
    ow_load.wait()

    @pl.loop(0, 2)
    def _(m):
        rows = pl.ds(m * half, half)
        S1[rows] = nn(ATT[pl.ds(T + m * half, half)], OW[...]).astype(BF)
        cross_rows(S1, 0, X1, 0, 3, m).start()

    attend(0)

    @pl.loop(0, 2)
    def _(m):
        rows = pl.ds(m * half, half)
        MID[rows] = nn(ATT[rows], OW[...])
        cross_rows(S1, 0, X1, 0, 3, m).wait()

        @pl.loop(0, half // 128)
        def _(q):
            rows = pl.ds(m * half + q * 128, 128)
            mid = TOKX[rows].astype(F32) + (MID[rows] + X1[rows].astype(F32) + obias[...])
            MID[rows] = mid
            N2[rows] = (normed(mid)[0] * gain2[...] + shift2[...]).astype(BF)

        cross_rows(N2, 0, N2, T, 5, m).start()

    SB[...] = jnp.zeros_like(SB)
    SB[15:16] = jnp.sum(CG[0:T].astype(F32), axis=0, keepdims=True)
    turned(T2, N2, 0, T)
    cot_send.wait()
    turned(T1, CG, T, T)

    @pl.loop(0, 2)
    def _(m):
        cross_rows(N2, 0, N2, T, 5, m).wait()

    turned(T2, N2, T, T)
    uw_load.wait()
    dw_load.wait()

    ones8 = jnp.ones((8, R), BF)

    wide = 2 * FC

    @pl.loop(0, nf // 2)
    def _(j):
        cols = pl.ds(pl.multiple_of(j * wide, wide), wide)

        @pl.loop(0, R // 256)
        def _(m):
            rows = pl.ds(m * 256, 256)
            h = nn(N2[rows], U[:, cols]) + ubias[:, cols]
            cdf = 0.5 + 0.5 * lax.erf(h * math.sqrt(0.5))
            ACT[rows, cols] = (h * cdf).astype(BF)
            slope = cdf + h * jnp.exp(h * h * -0.5) * (1.0 / math.sqrt(2 * math.pi))
            GH[rows, cols] = (nt(CG[rows], DN[cols]) * slope).astype(BF)

        poll("hidden", j)
        for k, (left, right) in enumerate(((T1, ACT), (T2, GH))):
            @pl.loop(0, D // 512)
            def _(m):
                both = nn(left[pl.ds(m * 512, 512)], right[:, cols])
                for e in range(2):
                    put("M", (2 * j + e, k), both[:, e * FC : (e + 1) * FC], m, M_KINDS[2 * e + k], j % 2)

            for e in range(2):
                rs_start("M", (2 * j + e, k), 0, order_of(M_KINDS[2 * e + k], j % 2))
            poll("down" if k == 0 else "up", j)

        sums = nn(ones8, GH[:, cols])
        per = D // wide
        SB[pl.ds(11 + core * (F // D) + j // per, 1), pl.ds(pl.multiple_of((j % per) * wide, wide), wide)] = sums[0:1]
    tok_again.start()

    def norm_back(g, x, gain, row):
        xhat, inv = normed(x)
        SB[row : row + 1] += jnp.sum(g * xhat, axis=0, keepdims=True)
        SB[row + 1 : row + 2] += jnp.sum(g, axis=0, keepdims=True)
        gx = g * gain
        a = jnp.mean(gx, axis=1, keepdims=True)
        b = jnp.mean(gx * xhat, axis=1, keepdims=True)
        return inv * (gx - a - xhat * b)

    @pl.loop(0, 2)
    def _(m):
        S1[pl.ds(m * half, half)] = nt(GH[pl.ds(T + m * half, half)], U[...]).astype(BF)
        cross_rows(S1, 0, X1, 0, 7, m).start()

    poll("norm")

    @pl.loop(0, 2)
    def _(m):
        WIDE[0] = nt(GH[pl.ds(m * half, half)], U[...])
        cross_rows(S1, 0, X1, 0, 7, m).wait()

        @pl.loop(0, half // 64)
        def _(q):
            at = pl.ds(m * half + q * 64, 64)
            g = WIDE[0, pl.ds(q * 64, 64)] + X1[at].astype(F32)
            total = CG[at].astype(F32) + norm_back(g, MID[at], gain2[...], 9)
            high = total.astype(BF)
            CG[at] = high
            TOKX[at] = (total - high.astype(F32)).astype(BF)
            SB[8:9] += jnp.sum(high.astype(F32), axis=0, keepdims=True)

        cross_rows(CG, 0, CG, T, 9, m).start()
        poll("branch", m)

    for c in pw_again:
        c.start()

    def grad_attended(m):
        rows = pl.ds(m * half, half)
        GH[rows, 0:E] = nt(CG[rows], OW[...]).astype(BF)

    @pl.loop(0, 2)
    def _(m):
        grad_attended(m)

    turned(T1, CG, 0, T)
    poll("attended")

    @pl.loop(0, 2)
    def _(m):
        cross_rows(CG, 0, CG, T, 9, m).wait()
        grad_attended(2 + m)

    turned(T1, CG, T, T)

    @pl.loop(0, D // 512)
    def _(m):
        both = nn(T1[pl.ds(m * 512, 512)], ATT[...])
        for c in range(2):
            put("O", c, both[:, c * FC : (c + 1) * FC], m, O_KINDS[c], 0)

    for c in range(2):
        rs_start("O", c, 0, order_of(O_KINDS[c], 0))
    turned(T2, N1, 0, R)
    poll("out")

    def sums(g, s):
        who = (partner(1 << s), core) if s < stages else (me, 1 - core)
        return pltpu.make_async_remote_copy(
            src_ref=SB.at[pl.ds(8 * g, 8)], dst_ref=SBR.at[g, s],
            send_sem=b_send.at[g, s], recv_sem=b_recv.at[g, s],
            device_id=who, device_id_type=MESH,
        )

    def sum_start(g, s):
        sums(g, s).start()

    def sum_step(g, s):
        sums(g, s).wait()
        SB[8 * g : 8 * g + 8] = SB[8 * g : 8 * g + 8] + SBR[g, s]
        if s < stages:
            sum_start(g, s + 1)

    def key_grads(b, k):
        return pl.ds(pl.multiple_of((2 * b + k) * LANES, LANES), LANES)

    sum_start(1, 0)
    @pl.loop(0, pairs)
    def _(p):
        cols = pl.ds(pl.multiple_of(p * LANES, LANES), LANES)
        key_sets(p, T1)
        N1[0:LANES] = K[:, cols].T
        for e in range(2):
            @pl.loop(0, R // 256)
            def _(b):
                rows = pl.ds(b * 256, 256)
                g = GH[rows, cols]
                both = g.astype(F32) * ATT[rows, cols].astype(F32)
                inner = jnp.sum(jnp.where(mine(e), both, 0.0), axis=1, keepdims=True)
                hi, mid, lo = split3(inner)
                feature = lane % HEAD
                terms = jnp.where(feature == TERM, -hi, jnp.where(feature == TERM + 1, -mid, -lo))
                is_term = (feature >= TERM) & (feature < TERM + 3)
                terms = jnp.where(is_term, terms, 0.0).astype(BF)
                T1[rows, (4 + e) * LANES : (5 + e) * LANES] = jnp.where(mine(e), g, terms)

        for e in range(2):
            WIDE[1, e * HEAD : (e + 1) * HEAD] = jnp.zeros((HEAD, R), F32)

        poll("keys", p)

        @pl.loop(0, R // 256)
        def _(b):
            rows = pl.ds(b * 256, 256)
            pair = []
            for e in range(2):
                dk = dv = 0.0
                for a in range(2):
                    across = pl.ds(a * T, T)
                    qa = QA[2 * p + e, across]
                    ga = T1[across, (4 + e) * LANES : (5 + e) * LANES]
                    w = jnp.exp(nt(T1[rows, e * LANES : (e + 1) * LANES], qa))
                    ds = (w * nt(T1[rows, (2 + e) * LANES : (3 + e) * LANES], ga)).astype(BF)
                    dv += nn(w.astype(BF), ga)
                    dk += nn(ds, qa)
                    WIDE[1, e * HEAD : (e + 1) * HEAD, across] += nn(N1[e * HEAD : (e + 1) * HEAD, rows], ds)
                pair.append((dk, dv))
            for k, (g0, g1) in enumerate(zip(*pair)):
                WIDE[0, :, key_grads(b, k)] = jnp.where(mine(0), g0, g1)
            poll("inner", p * (R // 256) + b)

        @pl.loop(0, R // 256)
        def _(b):
            rows = pl.ds(b * 256, 256)
            cos, sin = rotary(rows)

            def back(g):
                g = g.astype(BF).astype(F32)
                return g * cos - partner_of(g, lane) * sin

            parts = (
                back(WIDE[1, 0:LANES, rows].T) * HEAD**-0.5,
                back(WIDE[0, :, key_grads(b, 0)]),
                WIDE[0, :, key_grads(b, 1)],
            )
            for c, part in enumerate(parts):
                GH[rows, pl.ds(pl.multiple_of(E + (3 * p + c) * LANES, LANES), LANES)] = part.astype(BF)

        own_cols = pl.ds(pl.multiple_of(E + 3 * p * LANES, LANES), 3 * LANES)

        @pl.loop(0, D // 512)
        def _(m):
            three = nn(T2[pl.ds(m * 512, 512)], GH[:, own_cols])
            for c in range(3):
                put("P", (p, c), three[:, c * LANES : (c + 1) * LANES], m, P_KINDS[c], p % 2)

        for c in range(3):
            rs_start("P", (p, c), 0, order_of(P_KINDS[c], p % 2))
        totals = nn(ones8, GH[:, own_cols])[0:1]
        for c in range(3):
            at = pl.multiple_of(core * E + p * LANES, LANES)
            SB[2 + c : 3 + c, pl.ds(at, LANES)] = totals[:, c * LANES : (c + 1) * LANES]

        poll("pair", p)
        for q in range(min(pairs, stages + 1)):
            @pl.when(p == q)
            def _():
                sum_step(1, q)

    for c in pw_again:
        c.wait()

    @pl.loop(0, 2)
    def _(m):
        S1[pl.ds(m * half, half)] = nt(GH[pl.ds(T + m * half, half), E : 4 * E], U[:, : 3 * E]).astype(BF)
        cross_rows(S1, 0, X1, 0, 13, m).start()

    poll("input")
    tok_again.wait()

    @pl.loop(0, 2)
    def _(m):
        rows = pl.ds(m * half, half)
        WIDE[m] = nt(GH[rows, E : 4 * E], U[:, : 3 * E])
        cross_rows(S1, 0, X1, 0, 13, m).wait()

        @pl.loop(0, half // 64)
        def _(q):
            at = pl.ds(m * half + q * 64, 64)
            here = pl.ds(q * 64, 64)
            g = WIDE[m, here] + X1[at].astype(F32)
            before = CG[at].astype(F32) + TOKX[at].astype(F32)
            WIDE[m, here] = before + norm_back(g, N2[at].astype(F32), gain1[...], 0)


        gtok_store(m).start()

    sum_start(0, 0)

    poll("tokens")

    @pl.loop(0, 2)
    def _(m):
        S1[pl.ds(m * half, half)] = nn(ACT[pl.ds(T + m * half, half)], DN[...]).astype(BF)
        cross_rows(S1, 0, N2, T, 11, m).start()

    early = list(range(pairs, stages + 1))
    if early:
        sum_step(1, early.pop(0))
    sum_step(0, 0)
    poll("mixed")

    @pl.loop(0, 2)
    def _(m):
        rows = pl.ds(m * half, half)
        MID[rows] += nn(ACT[rows], DN[...])
        cross_rows(S1, 0, N2, T, 11, m).wait()

        @pl.loop(0, half // 64)
        def _(q):
            at = pl.ds(m * half + q * 64, 64)
            other = N2[pl.ds(T + m * half + q * 64, 64)].astype(F32)
            N2[at] = (MID[at] + (other + dbias[...])).astype(BF)

    mixed_store.start()
    for s in range(1, stages + 1):
        if early:
            sum_step(1, early.pop(0))
        sum_step(0, s)
        poll("last%d" % s)
    poll("rest")
    assert not plan
    small[...] = SB[...]
    mixed_store.wait()
    for m in range(2):
        gtok_store(m).wait()


def pieces_of(shapes):
    parts = []
    for k, shape in enumerate(shapes):
        n = math.gcd(shape[0], 64)
        parts += [(k, at, n) for at in range(0, shape[0], n)]
    return parts


def hand_over(*refs):
    parts = pieces_of([ref.shape for ref in refs[:6]])
    arrive, leave = [], []
    for q, (k, at, n) in enumerate(parts):
        rows = pl.ds(at, n)
        arrive.append(pltpu.make_async_copy(refs[k].at[rows], refs[-8 + k].at[rows], refs[-2].at[q]))
        leave.append(pltpu.make_async_copy(refs[-8 + k].at[rows], refs[7 + k].at[rows], refs[-1].at[q]))
    for c in arrive:
        c.start()
    small, vectors = refs[6], refs[13:21]
    for v, at in zip(vectors, (0, 1, 8, 9, 10, 15)):
        v[...] = small[at : at + 1]
    vectors[6][...] = small[2:5]
    for k in range(4):
        vectors[7][:, k * small.shape[1] : (k + 1) * small.shape[1]] = small[11 + k : 12 + k]
    for before, after in zip(arrive, leave):
        before.wait()
        after.start()
    for c in leave:
        c.wait()


M_KINDS = ("xyz", "yzx", "zxy", "yxz")
O_KINDS = ("xyz", "yzx")
P_KINDS = ("xyz", "yxz", "zxy")


def kind_of(fam, c):
    if fam == "M":
        return M_KINDS[2 * (c[0] % 2) + c[1]], (c[0] // 2) % 2
    if fam == "O":
        return O_KINDS[c], 0
    return P_KINDS[c[1]], c[0] % 2


def make_plan(stages, nf, pairs):
    now, free, flying, plan = 0.0, {}, {}, {}

    def send(fam, c, s):
        kind, par = kind_of(fam, c)
        axes = [a if not par or a == "z" else "yx"["xy".index(a)] for a in kind] + ["z"] + ["w"] * stages
        size = (FC if fam != "P" else LANES) / FC * WIRE / 2**s
        begin = max(now, free.get(axes[s], 0.0))
        free[axes[s]] = begin + size
        flying[(fam, c, s)] = begin + size + LATENCY

    def take(point, at, only=None, everything=False):
        nonlocal now
        while True:
            ready = [
                (t, k) for k, t in flying.items()
                if (everything or t <= now + SLACK or (only and only(k))) and (only is None or only(k))
            ]
            if not ready:
                return
            t, k = min(ready)
            del flying[k]
            now = max(now, t) + STEP
            plan.setdefault((point, at), []).append(k)
            if k[2] < stages - 1:
                send(k[0], k[1], k[2] + 1)

    def first(k):
        return k[0] == "M" and k[2] == 0

    for j in range(nf // 2):
        now += TIMES["hidden"]
        take("hidden", j, lambda k: first(k) and k[1][0] // 2 <= j - 2)
        take("hidden", j)
        for k, point in enumerate(("down", "up")):
            now += TIMES[point]
            for e in range(2):
                send("M", (2 * j + e, k), 0)
            take(point, j)
    now += TIMES["norm"]
    take("norm", 0)
    for m in range(2):
        now += TIMES["branch"]
        take("branch", m)
    now += TIMES["attended"]
    take("attended", 0, lambda k: first(k) and k[1][0] == nf - 3)
    take("attended", 0)
    now += TIMES["out"]
    for c in range(2):
        send("O", c, 0)
    take("out", 0)
    for p in range(pairs):
        now += TIMES["keys"]
        if p == 0:
            take("keys", p, first)
        if p == 2:
            take("keys", p, lambda k: k[0] == "O" and k[2] == 0)
        take("keys", p)
        for b in range(4):
            now += TIMES["inner"]
            take("inner", 4 * p + b)
        now += TIMES["pair"]
        for c in range(3):
            send("P", (p, c), 0)
        take("pair", p)
    for point in ("input", "tokens", "mixed"):
        now += TIMES[point]
        take(point, 0)
    now += TIMES["last"]
    for s in range(1, stages + 1):
        now += 2.0
        take("last%d" % s, 0)
    take("rest", 0, everything=True)
    return plan


WIRE = 8.5
LATENCY = 5.0
SLACK = 0.0
STEP = 0.3
TIMES = dict(
    hidden=3.0, down=1.5, up=1.6, norm=2.6, branch=2.5, attended=1.8, out=4.0, keys=2.4, inner=1.7,
    pair=3.0, input=1.8, tokens=4.0, mixed=2.6, last=3.0,
)


def on_device(
    tokens, episode_lengths, attn_gain, attn_shift, proj_weight, proj_bias, out_weight, out_bias,
    mlp_gain, mlp_shift, up_weight, up_bias, down_weight, down_bias, cotangent,
):
    dp = lax.axis_size("dp")
    stages = dp.bit_length() - 1
    T, D = tokens.shape
    R = 2 * T
    E = proj_weight.shape[2]
    F = up_weight.shape[1]
    pairs = E // LANES
    nf = F // FC
    row = lambda v: v.reshape(1, -1).astype(F32)
    rows_at = [max(D >> (s + 1), 16) for s in range(stages)]
    vmem = pl.BlockSpec(memory_space=pltpu.VMEM)
    hbm = pl.BlockSpec(memory_space=pl.ANY)
    smem = pl.BlockSpec(memory_space=pltpu.SMEM)
    dma = pltpu.SemaphoreType.DMA
    scratch = [
        pltpu.VMEM((D, F), BF),
        pltpu.VMEM((F, D), BF),
        pltpu.VMEM((E, D), BF),
        pltpu.VMEM((T, D), BF),
        pltpu.VMEM((R, D), BF),
        pltpu.VMEM((D, R), BF),
        pltpu.VMEM((D, R), BF),
        pltpu.VMEM((R, D), BF),
        pltpu.VMEM((R, D), BF),
        pltpu.VMEM((2 * pairs, R, LANES), BF),
        pltpu.VMEM((R, E), BF),
        pltpu.VMEM((R, E), BF),
        pltpu.VMEM((R, E), BF),
        pltpu.VMEM((R, F), BF),
        pltpu.VMEM((R, F), BF),
        pltpu.VMEM((T, D), F32),
        pltpu.VMEM((T, D), BF),
        pltpu.VMEM((T, D), BF),
        pltpu.VMEM((R, LANES), BF),
        pltpu.VMEM((R, LANES), BF),
        pltpu.VMEM((R, LANES), BF),
        pltpu.VMEM((16, D), F32),
        pltpu.VMEM((2, stages + 1, 8, D), F32),
        pltpu.VMEM((2, T // 2, D), F32),
        pltpu.VMEM((8, D, FC), BF),
        *[pltpu.VMEM((2 * nf + 2, n, FC), BF) for n in rows_at],
        *[pltpu.VMEM((3 * pairs, n, LANES), BF) for n in rows_at],
        dma((2 * nf + 2, stages)), dma((2 * nf + 2, stages)),
        dma((3 * pairs, stages)), dma((3 * pairs, stages)),
        dma((15,)), dma((15,)), dma((2, stages + 1)), dma((2, stages + 1)), dma((10 + 6 * pairs,)),
    ]
    n = D // dp
    struct = jax.ShapeDtypeStruct
    made = pl.pallas_call(
        functools.partial(kernel, dp),
        out_shape=(
            struct((T, D), BF), struct((T, D), F32), struct((n, F), F32), struct((n, F), F32),
            struct((n, E), F32), struct((3, n, E), F32), struct((16, D), F32),
        ),
        in_specs=[hbm] * 6 + [smem] + [vmem] * 9,
        out_specs=(hbm, hbm, vmem, vmem, vmem, vmem, vmem),
        scratch_shapes=scratch,
        compiler_params=pltpu.CompilerParams(
            collective_id=0, has_side_effects=True, vmem_limit_bytes=63 << 20
        ),
        name="block",
    )(
        tokens, cotangent, proj_weight, out_weight, up_weight, down_weight, episode_lengths,
        row(attn_gain), row(attn_shift), proj_bias, row(out_bias), row(mlp_gain), row(mlp_shift),
        row(up_bias), row(down_bias), jnp.asarray(rope_tables()),
    )
    parts = len(pieces_of([v.shape for v in made[:6]]))
    vectors = [struct((1, D), F32)] * 6 + [struct((3, D), F32), struct((1, 4 * D), F32)]
    mixed, grad_tokens, down, up, out, proj, gain1, shift1, obias, gain2, shift2, dbias, pbias, ubias = pl.pallas_call(
        hand_over,
        out_shape=tuple(struct(v.shape, v.dtype) for v in made[:6]) + tuple(vectors),
        in_specs=[hbm] * 6 + [vmem],
        out_specs=(hbm,) * 6 + (vmem,) * 8,
        scratch_shapes=[*(pltpu.VMEM(v.shape, v.dtype) for v in made[:6]), dma((parts,)), dma((parts,))],
        name="outputs",
    )(*made)
    return (
        mixed, grad_tokens, gain1[0], shift1[0], proj, pbias, out.T, obias[0], gain2[0], shift2[0],
        up, ubias.reshape(-1), down.T, dbias[0],
    )


def solution(mesh):
    rows = P(("dp", "tensor"), None)
    return jax.shard_map(
        on_device,
        mesh=mesh,
        in_specs=(
            rows, P("dp", None), P(), P(), P(None, None, "tensor"), P(None, "tensor"), P("tensor", None), P(),
            P(), P(), P(None, "tensor"), P("tensor"), P("tensor", None), P(), rows,
        ),
        out_specs=(
            rows, rows, P(), P(), P(None, "dp", "tensor"), P(), P("tensor", "dp"), P(), P(), P(),
            P("dp", "tensor"), P(), P("tensor", "dp"), P(),
        ),
        check_vma=False,
    )
```
